128 devices in a mesh: fsdp: 64 (over z, x_hi, y, core), seq: 2 (over x_lo).
Axes of the slice: x: 4 (x_hi: 2, x_lo: 2; x = x_hi * 2 + x_lo), y: 4, z: 4, core: 2. Of those that a mesh axis runs over, the one named last changes fastest.
Arguments:
- inputs: bfloat16 [2, 64, 580, 768], P(None, 'fsdp', 'seq'), may hold values from -6 to 6
- cotangent: bfloat16 [2, 64, 580, 768], P(None, 'fsdp', 'seq'), may hold values from -6 to 6
- lengths: int32 [2, 64], P(None, 'fsdp'), may hold values from 291 to 580, as said below
- w_qkv: bfloat16 [768, 2304], P(('fsdp', 'seq')), may hold values from -0.21875 to 0.21875
- w_out: bfloat16 [768, 768], P(('fsdp', 'seq')), may hold values from -2.5 to 2.5
- w_up: bfloat16 [768, 3072], P(('fsdp', 'seq')), may hold values from -0.21875 to 0.21875
- w_down: bfloat16 [3072, 768], P(('fsdp', 'seq')), may hold values from -0.109375 to 0.109375
- ln1_gain: bfloat16 [768], P(('fsdp', 'seq')), may hold values from 0.5 to 1.5
- ln1_shift: bfloat16 [768], P(('fsdp', 'seq')), may hold values from -4 to 4
- q_bias: bfloat16 [768], P(('fsdp', 'seq')), may hold values from -4 to 4
- v_bias: bfloat16 [768], P(('fsdp', 'seq')), may hold values from -4 to 4
- out_bias: bfloat16 [768], P(('fsdp', 'seq')), may hold values from -4 to 4
- ln2_gain: bfloat16 [768], P(('fsdp', 'seq')), may hold values from 0.5 to 1.5
- ln2_shift: bfloat16 [768], P(('fsdp', 'seq')), may hold values from -4 to 4
- up_bias: bfloat16 [3072], P(('fsdp', 'seq')), may hold values from -4 to 4
- down_bias: bfloat16 [768], P(('fsdp', 'seq')), may hold values from -4 to 4
Outputs:
- outputs: bfloat16 [2, 64, 580, 768], P(None, 'fsdp', 'seq')
- input_grad: float32 [2, 64, 580, 768], P(None, 'fsdp', 'seq')
- grad_w_qkv: float32 [768, 2304], P(('fsdp', 'seq'))
- grad_w_out: float32 [768, 768], P(('fsdp', 'seq'))
- grad_w_up: float32 [768, 3072], P(('fsdp', 'seq'))
- grad_w_down: float32 [3072, 768], P(('fsdp', 'seq'))
- grad_ln1_gain: float32 [768], P(('fsdp', 'seq'))
- grad_ln1_shift: float32 [768], P(('fsdp', 'seq'))
- grad_q_bias: float32 [768], P(('fsdp', 'seq'))
- grad_v_bias: float32 [768], P(('fsdp', 'seq'))
- grad_out_bias: float32 [768], P(('fsdp', 'seq'))
- grad_ln2_gain: float32 [768], P(('fsdp', 'seq'))
- grad_ln2_shift: float32 [768], P(('fsdp', 'seq'))
- grad_up_bias: float32 [3072], P(('fsdp', 'seq'))
- grad_down_bias: float32 [768], P(('fsdp', 'seq'))
The draws below stay inside these ranges and needn't reach their ends.
Inputs may be any that keep to these rules, and one draw needn't show every extreme that they name: `lengths`: keys at or after an image's length are masked; some image is full and some has the fewest.
All inputs are finite; a program needn't handle non-finite values.
Results may differ from the reference program's by a relative error of at most 0.012.
Values may be sent and summed in bfloat16 or wider, within the bound.
No kernel may reach another device: no remote copies, remote signals or barrier semaphores. Data moves between devices by JAX's collectives and lax.ppermute only.
A program may use at most 256 MiB of HBM per device.

```python
import math
import jax
import jax.numpy as jnp
from jax import lax

D = 768
HEADS = 12
HDIM = 64
FF = 3072
LPAD = 580
MICRO = 2
TOK_DEV = 290
NIMG = 64


def draw_lengths(key, part):
    key = jax.random.fold_in(key, 7)
    first_key, second_key, third_key = jax.random.split(key, 3)
    lowest = LPAD - TOK_DEV + 1
    lengths_drawn = jax.random.randint(first_key, (MICRO * NIMG,), lowest, LPAD + 1)
    longest = jax.random.randint(second_key, (), 0, MICRO * NIMG)
    offset = jax.random.randint(third_key, (), 1, MICRO * NIMG)
    shortest = (longest + offset) % (MICRO * NIMG)
    slot_ids = jnp.arange(MICRO * NIMG)
    lengths_drawn = jnp.where(slot_ids == longest, LPAD, lengths_drawn)
    lengths_drawn = jnp.where(slot_ids == shortest, lowest, lengths_drawn)
    return lengths_drawn.reshape(MICRO, NIMG).astype(jnp.int32)


def shard_levels(own_key, shape, pieces, least, largest):
    level, own = 1.0, jax.random.fold_in(own_key, 6)
    for dim, parts in pieces:
        steps = jnp.exp(jax.random.uniform(jax.random.fold_in(own, dim), (parts,), jnp.float32, least / len(pieces), largest / len(pieces)))
        level = level * jnp.repeat(steps, shape[dim] // parts).reshape([-1 if axis == dim else 1 for axis in range(len(shape))])
    return level


def gaussian(stream_key, dims, scale, bound, cuts=(), kind=jnp.bfloat16):
    array = jax.random.normal(stream_key, dims, jnp.float32) * scale
    if len(cuts) > 0:
        array = shard_levels(stream_key, dims, cuts, -0.22, 0.18) * array
    return jnp.clip(array, min=-bound, max=bound).astype(kind)


def setup_inputs(seed: int = 0) -> dict:
    key_of = jax.random.split(jax.random.key(seed), 17)
    return {
        "inputs": gaussian(key_of[0], (MICRO, NIMG, LPAD, D), 1.0, 6.0, ((1, 64), (2, 2))),
        "cotangent": gaussian(key_of[1], (MICRO, NIMG, LPAD, D), 1.0, 6.0, ((1, 64), (2, 2))),
        "lengths": draw_lengths(jax.random.fold_in(key_of[16], 71), 0),
        "w_qkv": gaussian(key_of[3], (D, 3 * D), D ** -0.5, 0.21875, ((0, 128),)),
        "w_out": gaussian(key_of[4], (D, D), (max(1, 4 * D // LPAD)) ** -0.5, 2.5, ((0, 128),)),
        "w_up": gaussian(key_of[5], (D, FF), D ** -0.5, 0.21875, ((0, 128),)),
        "w_down": gaussian(key_of[6], (FF, D), FF ** -0.5, 0.109375, ((0, 128),)),
        "ln1_gain": jnp.clip(1.0 + 0.1 * jax.random.normal(key_of[7], (D,), jnp.float32), 0.5, 1.5).astype(jnp.bfloat16),
        "ln1_shift": gaussian(key_of[8], (D,), 0.3, 4.0, ((0, 128),)),
        "q_bias": gaussian(key_of[9], (D,), 0.5, 4.0, ((0, 128),)),
        "v_bias": gaussian(key_of[10], (D,), 0.5, 4.0, ((0, 128),)),
        "out_bias": gaussian(key_of[11], (D,), 0.5, 4.0, ((0, 128),)),
        "ln2_gain": jnp.clip(1.0 + 0.1 * jax.random.normal(key_of[12], (D,), jnp.float32), 0.5, 1.5).astype(jnp.bfloat16),
        "ln2_shift": gaussian(key_of[13], (D,), 0.3, 4.0, ((0, 128),)),
        "up_bias": gaussian(key_of[14], (FF,), 0.5, 4.0, ((0, 128),)),
        "down_bias": gaussian(key_of[15], (D,), 0.5, 4.0, ((0, 128),)),
    }


PRECISE = lax.Precision.HIGHEST

@jax.custom_vjp
def low(v):
    return lax.optimization_barrier(v.astype(jnp.bfloat16)).astype(jnp.float32)

@jax.custom_vjp
def low_back(v):
    return v

def low_keep(v):
    return (low(v), None)

def low_pass(kept, grad):
    return (grad,)

def back_keep(v):
    return (v, None)

def back_low(kept, grad):
    return (low(grad),)
low.defvjp(low_keep, low_pass)
low_back.defvjp(back_keep, back_low)

def norm_rows(values, gain_vec, shift_vec):
    average = lax.optimization_barrier(jnp.mean(values, axis=-1, keepdims=True))
    centred = values - average
    spread = lax.optimization_barrier(jnp.mean(centred * centred, axis=-1, keepdims=True))
    return centred * lax.rsqrt(spread + 1e-06) * gain_vec + shift_vec

def image_block(tokens_in, length, params):
    w_qkv, w_out, w_up, w_down, ln1_gain, ln1_shift, q_bias, v_bias, out_bias, ln2_gain, ln2_shift, up_bias, down_bias = params
    model_width = w_out.shape[0]
    normed = low(norm_rows(tokens_in, ln1_gain, ln1_shift))
    qkv_bias = jnp.concatenate([q_bias, jnp.zeros_like(q_bias), v_bias])
    joined = low(low_back(jnp.dot(normed, w_qkv, precision=PRECISE) + qkv_bias))
    queries = joined[:, :model_width].reshape(LPAD, HEADS, HDIM)
    keys_all = joined[:, model_width:2 * model_width].reshape(LPAD, HEADS, HDIM)
    values_all = joined[:, 2 * model_width:].reshape(LPAD, HEADS, HDIM)
    scores = jnp.einsum('qhd,khd->hqk', queries, keys_all, precision=PRECISE) * (1.0 / math.sqrt(HDIM))
    position = jnp.arange(LPAD, dtype=jnp.int32)
    scores = jnp.where((position < length)[None, None, :], scores, -1e+30)
    scores = low_back(scores)
    row_max = lax.optimization_barrier(jnp.max(scores, axis=-1, keepdims=True))
    exp_rows = jnp.exp(scores - row_max)
    soft_weights = low(exp_rows / lax.optimization_barrier(jnp.sum(exp_rows, axis=-1, keepdims=True)))
    attended = jnp.einsum('hqk,khd->qhd', soft_weights, values_all, precision=PRECISE).reshape(LPAD, model_width)
    attended = low(low_back(attended))
    branch = low_back(jnp.dot(attended, w_out, precision=PRECISE) + out_bias)
    middle = tokens_in + branch
    normed_two = low(norm_rows(middle, ln2_gain, ln2_shift))
    hidden = low_back(jnp.dot(normed_two, w_up, precision=PRECISE) + up_bias)
    active = low(jax.nn.gelu(hidden, approximate=False))
    result = low_back(jnp.dot(active, w_down, precision=PRECISE) + down_bias)
    return middle + result

def reference(inputs, cotangent, lengths, w_qkv, w_out, w_up, w_down, ln1_gain, ln1_shift, q_bias, v_bias, out_bias, ln2_gain, ln2_shift, up_bias, down_bias):
    params = tuple((element.astype(jnp.float32) for element in (w_qkv, w_out, w_up, w_down, ln1_gain, ln1_shift, q_bias, v_bias, out_bias, ln2_gain, ln2_shift, up_bias, down_bias)))
    flat_in = inputs.astype(jnp.float32).reshape(MICRO * NIMG, LPAD, D)
    flat_len = lengths.reshape(MICRO * NIMG).astype(jnp.int32)

    def forward(images, weights):

        def per_image(element):
            return image_block(element[0], element[1], weights)
        return lax.map(jax.checkpoint(per_image), (images, flat_len))
    results, pullback = jax.vjp(forward, flat_in, params)
    input_grad, grads = pullback(cotangent.astype(jnp.float32).reshape(MICRO * NIMG, LPAD, D))
    shape_out = (MICRO, NIMG, LPAD, D)
    return (results.reshape(shape_out).astype(jnp.bfloat16), input_grad.reshape(shape_out), grads[0], grads[1], grads[2], grads[3], grads[4], grads[5], grads[6], grads[7], grads[8], grads[9], grads[10], grads[11], grads[12])
```

```python
import math

import jax
import jax.numpy as jnp
from jax import lax
from jax.sharding import Mesh
from jax.sharding import PartitionSpec as P

HDIM = 64
D = 768
FF = 3072
HEADS = 12
TOK = 290
HALF = 304
ROWS = 2 * HALF
AXES = ("z", "xh", "y", "core", "xl")
CHIPS = ("z", "xh", "y", "xl")
BF = jnp.bfloat16
F32 = jnp.float32


def norm_rows(values, gain_vec, shift_vec):
    average = jnp.mean(values, axis=-1, keepdims=True)
    centred = values - average
    spread = jnp.mean(centred * centred, axis=-1, keepdims=True)
    inverse = lax.rsqrt(spread + 1e-06)
    unit_rows = centred * inverse
    return (unit_rows * gain_vec + shift_vec, unit_rows, inverse)


def norm_back(grad_rows, unit_rows, inverse, gain_vec):
    scaled = grad_rows * gain_vec
    mean_plain = jnp.mean(scaled, axis=-1, keepdims=True)
    mean_unit = jnp.mean(scaled * unit_rows, axis=-1, keepdims=True)
    grad_in = inverse * (scaled - mean_plain - unit_rows * mean_unit)
    return (grad_in, jnp.sum(grad_rows * unit_rows, axis=0), jnp.sum(grad_rows, axis=0))


def transposed(left, right):
    return jnp.einsum("ti,to->io", left, right, preferred_element_type=F32)


def times_transpose(left, right):
    return jnp.einsum("to,io->ti", left, right, preferred_element_type=F32)


def swap(value, axis):
    return lax.ppermute(value, axis, [(0, 1), (1, 0)])


def gather_wire(wire):
    n = wire.shape[0]
    mine = lax.all_to_all(jnp.broadcast_to(wire[None], (64, n, 128)), CHIPS, 0, 0, tiled=True)
    other = swap(mine, "core")
    mine = mine.reshape(32, 2, n, 128)
    other = other.reshape(32, 2, n, 128)
    first = lax.axis_index("core") == 0
    both = jnp.stack([jnp.where(first, mine, other), jnp.where(first, other, mine)], axis=1)
    return both.reshape(128, n, 128)


def reduce_wire(parts):
    n = parts.shape[1]
    parts = parts.reshape(32, 2, 2, n, 128)
    core = lax.axis_index("core")
    away = lax.dynamic_index_in_dim(parts, 1 - core, 1, keepdims=False).astype(BF)
    kept = lax.dynamic_index_in_dim(parts, core, 1, keepdims=False)
    both = (kept.astype(F32) + swap(away, "core").astype(F32)).astype(BF)
    spread = lax.all_to_all(both.reshape(64, n, 128), CHIPS, 0, 0, tiled=True)
    return jnp.sum(spread.astype(F32), axis=0)


def pad_wire(value, rows):
    return jnp.pad(value, ((0, 0),) * (value.ndim - 2) + ((0, rows - value.shape[-2]), (0, 0)))


def per_device(
    inputs,
    cotangent,
    lengths,
    w_qkv,
    w_out,
    w_up,
    w_down,
    ln1_gain,
    ln1_shift,
    q_bias,
    v_bias,
    out_bias,
    ln2_gain,
    ln2_shift,
    up_bias,
    down_bias,
):
    side = lax.axis_index("xl")
    scale_factor = 1.0 / math.sqrt(HDIM)

    smalls = jnp.concatenate(
        [ln1_gain, ln1_shift, q_bias, v_bias, out_bias, ln2_gain, ln2_shift, down_bias, up_bias]
    )
    smalls = jnp.pad(smalls, (0, 128 - 72)).reshape(1, 128)
    wire_one = pad_wire(jnp.concatenate([w_qkv.reshape(108, 128), smalls]), 112)
    wire_two = pad_wire(jnp.concatenate([w_out.reshape(36, 128), w_up.reshape(144, 128)]), 192)
    wire_three = w_down.reshape(144, 128)

    def own_image(block):
        mine = lax.dynamic_index_in_dim(block, side, 0, keepdims=False)[0]
        theirs = lax.dynamic_index_in_dim(block, 1 - side, 0, keepdims=False)[0]
        got = swap(theirs, "xl")
        return jnp.pad(jnp.stack([mine, got]), ((0, 0), (0, HALF - TOK), (0, 0))).reshape(ROWS, D)

    def give_back(rows):
        halves = rows.reshape(2, HALF, D)[:, :TOK]
        got = swap(halves[1].astype(BF), "xl").astype(rows.dtype)
        kept = halves[0]
        first = side == 0
        return jnp.stack([jnp.where(first, kept, got), jnp.where(first, got, kept)])[:, None]

    tokens_in = own_image(inputs).astype(F32)
    full_one = gather_wire(wire_one)
    grad_low = own_image(cotangent)
    grad_out = grad_low.astype(F32)
    full_two = gather_wire(wire_two)
    full_three = gather_wire(wire_three)

    full_qkv = full_one[:, :108].reshape(D, 3 * D)
    vecs = full_one[:, 108, :72].astype(F32)
    gain_one, shift_one, bias_query, bias_value, bias_out, gain_two, shift_two, bias_down = (
        vecs[:, 6 * i : 6 * i + 6].reshape(D) for i in range(8)
    )
    bias_up = vecs[:, 48:72].reshape(FF)
    full_out = full_two[:, :36].reshape(D, D)
    full_up = full_two[:, 36:180].reshape(D, FF)
    full_down = full_three.reshape(FF, D)

    slot = jnp.arange(ROWS, dtype=jnp.int32)
    within = slot % HALF
    half_id = (slot // HALF + side) % 2
    position = jnp.where(within < TOK, within + TOK * half_id, 2 * TOK)
    length = lax.dynamic_index_in_dim(lengths, side, 0, keepdims=False)[0]
    key_ok = position < length

    normed, unit_one, inv_one = norm_rows(tokens_in, gain_one, shift_one)
    normed_low = normed.astype(BF)
    qkv_bias = jnp.concatenate([bias_query, jnp.zeros_like(bias_query), bias_value])
    joined = (jnp.dot(normed_low, full_qkv, preferred_element_type=F32) + qkv_bias).astype(BF)
    queries, keys, values = (
        joined[:, i * D : (i + 1) * D].reshape(ROWS, HEADS, HDIM) for i in range(3)
    )

    def scored():
        scores = jnp.einsum("qhd,khd->hqk", queries, keys, preferred_element_type=F32)
        return jnp.where(key_ok[None, None, :], scores * scale_factor, -1e30)

    scores = scored()
    row_max = jnp.max(scores, axis=-1, keepdims=True)
    exp_rows = jnp.exp(scores - row_max)
    row_total = jnp.sum(exp_rows, axis=-1, keepdims=True)
    soft_low = (exp_rows / row_total).astype(BF)
    log_total = row_max + jnp.log(row_total)
    attended = jnp.einsum("hqk,khd->qhd", soft_low, values, preferred_element_type=F32)
    attended = attended.reshape(ROWS, D).astype(BF)
    middle = tokens_in + (jnp.dot(attended, full_out, preferred_element_type=F32) + bias_out)
    normed_two, unit_two, inv_two = norm_rows(middle, gain_two, shift_two)
    normed_two_low = normed_two.astype(BF)
    hidden = jnp.dot(normed_two_low, full_up, preferred_element_type=F32) + bias_up
    phi = 0.5 * (1.0 + lax.erf(hidden * math.sqrt(0.5)))
    active_low = (hidden * phi).astype(BF)
    slope = phi + hidden * (jnp.exp(-0.5 * hidden * hidden) * (1.0 / math.sqrt(2.0 * math.pi)))
    results = middle + (jnp.dot(active_low, full_down, preferred_element_type=F32) + bias_down)
    results = give_back(results.astype(BF))

    grad_shrink = transposed(active_low, grad_low)
    shrink_bias = jnp.sum(grad_out, axis=0)
    own_down = reduce_wire(grad_shrink.reshape(128, 144, 128))
    grad_hidden = (times_transpose(grad_low, full_down) * slope).astype(BF)
    grad_expand = transposed(normed_two_low, grad_hidden)
    expand_bias = jnp.sum(grad_hidden.astype(F32), axis=0)
    grad_middle_norm, second_gain, second_shift = norm_back(
        times_transpose(grad_hidden, full_up), unit_two, inv_two, gain_two
    )
    grad_middle = grad_out + grad_middle_norm
    branch_low = grad_middle.astype(BF)
    grad_project = transposed(attended, branch_low)
    project_bias = jnp.sum(branch_low.astype(F32), axis=0)
    own_two = reduce_wire(
        pad_wire(
            jnp.concatenate(
                [grad_project.reshape(128, 36, 128), grad_expand.reshape(128, 144, 128)], axis=1
            ),
            192,
        )
    )
    grad_attended = times_transpose(branch_low, full_out).astype(BF).reshape(ROWS, HEADS, HDIM)
    soft_weights = jnp.exp(scored() - log_total)
    grad_probs = jnp.einsum("qhd,khd->hqk", grad_attended, values, preferred_element_type=F32)
    grad_values = jnp.einsum(
        "hqk,qhd->khd", soft_weights.astype(BF), grad_attended, preferred_element_type=F32
    )
    row_inner = jnp.sum(soft_weights * grad_probs, axis=-1, keepdims=True)
    grad_scores = (soft_weights * (grad_probs - row_inner)).astype(BF)
    grad_queries = (
        jnp.einsum("hqk,khd->qhd", grad_scores, keys, preferred_element_type=F32) * scale_factor
    )
    grad_keys = (
        jnp.einsum("hqk,qhd->khd", grad_scores, queries, preferred_element_type=F32) * scale_factor
    )
    grad_joined = jnp.concatenate(
        [item.reshape(ROWS, D) for item in (grad_queries, grad_keys, grad_values)], axis=1
    ).astype(BF)
    grad_joint = transposed(normed_low, grad_joined)
    joined_sums = jnp.sum(grad_joined.astype(F32), axis=0)
    grad_normed_in, first_gain, first_shift = norm_back(
        times_transpose(grad_joined, full_qkv), unit_one, inv_one, gain_one
    )
    input_grad = give_back(grad_middle + grad_normed_in)

    small_list = (
        first_gain,
        first_shift,
        joined_sums[:D],
        joined_sums[2 * D :],
        project_bias,
        second_gain,
        second_shift,
        shrink_bias,
    )
    small_grads = jnp.concatenate(
        [item.reshape(128, 6) for item in small_list] + [expand_bias.reshape(128, 24)], axis=1
    )
    small_grads = jnp.pad(small_grads, ((0, 0), (0, 128 - 72))).reshape(128, 1, 128)
    own_one = reduce_wire(
        pad_wire(jnp.concatenate([grad_joint.reshape(128, 108, 128), small_grads], axis=1), 112)
    )
    own_small = own_one[108]
    return (
        results,
        input_grad,
        own_one[:108].reshape(6, 3 * D),
        own_two[:36].reshape(6, D),
        own_two[36:180].reshape(6, FF),
        own_down.reshape(24, D),
        own_small[0:6],
        own_small[6:12],
        own_small[12:18],
        own_small[18:24],
        own_small[24:30],
        own_small[30:36],
        own_small[36:42],
        own_small[48:72],
        own_small[42:48],
    )


def solution(mesh):
    fine = Mesh(mesh.devices.reshape(4, 2, 4, 2, 2), AXES)
    images = ("z", "xh", "y", "core")
    rows, vec = P(AXES, None), P(AXES)
    tokens = P(None, images, "xl", None)
    return jax.shard_map(
        per_device,
        mesh=fine,
        in_specs=(tokens, tokens, P(None, images)) + (rows,) * 4 + (vec,) * 9,
        out_specs=(tokens, tokens) + (rows,) * 4 + (vec,) * 9,
        check_vma=False,
    )
```

```python
import functools
import math

import jax
import jax.numpy as jnp
from jax import lax
from jax.experimental import pallas as pl
from jax.experimental.pallas import tpu as pltpu
from jax.sharding import Mesh
from jax.sharding import PartitionSpec as P

D = 768
FF = 3072
TOK = 290
HALF = 320
ROWS = 2 * HALF
AXES = ("z", "xh", "y", "core", "xl")
BF = jnp.bfloat16
F32 = jnp.float32
F2C = 640
B2C = 640
SUB = 768
FFC = 640
VFF = 60


def mm(a, b):
    return lax.dot_general(a, b, (((1,), (0,)), ((), ())), preferred_element_type=F32)


def mm_nt(a, b):
    return lax.dot_general(a, b, (((1,), (1,)), ((), ())), preferred_element_type=F32)


def mm_tn(a, b):
    return lax.dot_general(a, b, (((0,), (0,)), ((), ())), preferred_element_type=F32)


def unit(values):
    centred = values - jnp.mean(values, axis=-1, keepdims=True)
    inverse = lax.rsqrt(jnp.mean(centred * centred, axis=-1, keepdims=True) + 1e-06)
    return centred * inverse, inverse


def norm_back(e, u, inverse, gain):
    s = e * gain
    mean = jnp.mean(s, axis=-1, keepdims=True)
    return inverse * (s - mean - u * jnp.mean(s * u, axis=-1, keepdims=True))


def call(kernel, meta, grid, ins, outs, scratch=(), us=10, vmem=60):
    return pl.pallas_call(
        kernel,
        grid_spec=pltpu.PrefetchScalarGridSpec(
            num_scalar_prefetch=1,
            grid=grid,
            in_specs=[spec for spec, _ in ins],
            out_specs=[spec for spec, _ in outs],
            scratch_shapes=list(scratch),
        ),
        out_shape=[shape for _, shape in outs],
        cost_estimate=pl.CostEstimate(
            flops=us * 10**9, bytes_accessed=us * 3 * 10**6, transcendentals=0
        ),
        compiler_params=pltpu.CompilerParams(vmem_limit_bytes=vmem * 2**20),
    )(meta, *[array for _, array in ins])


def whole(shape):
    return pl.BlockSpec(shape, lambda *_: (0,) * len(shape))


def sds(shape, dt):
    return jax.ShapeDtypeStruct(shape, dt)


def mine_spec(n):
    return pl.BlockSpec((4, 1, 192, n), lambda j, m: (0, jnp.clip(j - 2 * m[0], 0, 1), 0, 0))


def other_spec(n):
    return pl.BlockSpec((4, 1, 192, n), lambda j, m: (0, jnp.clip(j - 2 + 2 * m[0], 0, 1), 0, 0))


def rows_of(ref, i=0):
    return ref[:, i].reshape(D, ref.shape[-1])


OWN_HALF = pl.BlockSpec((1, 1, TOK, D), lambda j, m: (m[1], 0, 0, 0))
FULL = whole((ROWS, D))


def fill(ref, mine, got):
    ref[0:TOK] = mine
    ref[TOK:HALF] = jnp.zeros((HALF - TOK, D), BF)
    ref[HALF : HALF + TOK] = got
    ref[HALF + TOK :] = jnp.zeros((HALF - TOK, D), BF)


def key_ok(meta, shape, axis):
    slot = lax.broadcasted_iota(jnp.int32, shape, axis)
    half = (slot >= HALF).astype(jnp.int32)
    within = slot - half * HALF
    half = jnp.where(meta[1] == 1, 1 - half, half)
    return jnp.where((within < TOK) & (within + TOK * half < meta[2]), 0.0, -1e30).astype(F32)


def f1_kernel(meta, x_ref, got_ref, sm_ref, so_ref, wm_ref, wo_ref, qkv_ref, n1_ref, vec_ref, im_ref, bias_ref):
    j = pl.program_id(0)

    @pl.when(j == 0)
    def _():
        small = jnp.where(meta[0] == 1, rows_of(sm_ref).astype(F32), rows_of(so_ref).astype(F32))
        vec = small.T[:16]
        vec_ref[...] = vec
        fill(im_ref, x_ref[0, 0], got_ref[...])
        u, _ = unit(im_ref[...].astype(F32))
        n1_ref[...] = (u * vec[0:1] + vec[1:2]).astype(BF)
        bias_ref[...] = jnp.zeros_like(bias_ref)
        bias_ref[0:1, 0:D] = vec[2:3]
        bias_ref[0:1, 2 * D : 3 * D] = vec[3:4]

    b = bias_ref[0:1, pl.ds(pl.multiple_of(j * 640, 128), 640)]
    own = (j // 2) == meta[0]

    @pl.when(own)
    def _():
        qkv_ref[...] = (mm(n1_ref[...], rows_of(wm_ref)) + b).astype(BF)

    @pl.when(jnp.logical_not(own))
    def _():
        qkv_ref[...] = (mm(n1_ref[...], rows_of(wo_ref)) + b).astype(BF)


def f1(meta, x, got, mine, other):
    tail = pl.BlockSpec((4, 1, 192, 128), lambda j, m: (0, 1, 0, 3))
    return call(
        f1_kernel,
        meta,
        (4,),
        [(OWN_HALF, x), (whole((TOK, D)), got), (tail, mine), (tail, other)]
        + [(mine_spec(640), mine), (other_spec(640), other)],
        [
            (pl.BlockSpec((ROWS, 640), lambda j, m: (0, j)), sds((ROWS, 2560), BF)),
            (FULL, sds((ROWS, D), BF)),
            (whole((16, D)), sds((16, D), F32)),
            (FULL, sds((ROWS, D), BF)),
        ],
        [pltpu.VMEM((8, 2560), F32)],
        us=6,
        vmem=24,
    )


def head_block(first):
    return pl.BlockSpec((ROWS, 128), lambda h, m: (0, h + first))


def f2_kernel(meta, q_ref, k_ref, v_ref, o_ref, lse_ref):
    lane0 = lax.broadcasted_iota(jnp.int32, (1, 128), 1) < 64
    k = k_ref[...]
    v = v_ref[...]
    mask = key_ok(meta, (1, ROWS), 1)
    for c in range(0, ROWS, F2C):
        q = q_ref[c : c + F2C] * jnp.asarray(0.125, BF)
        res = []
        for pick in (lane0, ~lane0):
            s = mm_nt(jnp.where(pick, q, jnp.zeros_like(q)), k) + mask
            top = jnp.max(s, axis=-1, keepdims=True)
            p = jnp.exp(s - top)
            total = jnp.sum(p, axis=-1, keepdims=True)
            o = mm(p.astype(BF), v) * (1.0 / total)
            res.append((o, jnp.broadcast_to(top + jnp.log(total), (F2C, 128))))
        o_ref[c : c + F2C] = jnp.where(lane0, res[0][0], res[1][0]).astype(BF)
        lse_ref[c : c + F2C] = jnp.where(lane0, res[0][1], res[1][1])


def f2(meta, qkv):
    return call(
        f2_kernel,
        meta,
        (6,),
        [(head_block(0), qkv), (head_block(6), qkv), (head_block(12), qkv)],
        [(head_block(0), sds((ROWS, D), BF)), (head_block(0), sds((ROWS, D), F32))],
        us=12,
        vmem=24,
    )


def b2_kernel(meta, q_ref, k_ref, v_ref, do_ref, o_ref, lse_ref, dq_ref, dk_ref, dv_ref):
    lane0 = lax.broadcasted_iota(jnp.int32, (1, 128), 1) < 64
    q = q_ref[...] * jnp.asarray(0.125, BF)
    do = do_ref[...]
    lse = lse_ref[...].T
    dd = (do.astype(F32) * o_ref[...].astype(F32)).T
    mask_all = key_ok(meta, (ROWS, 1), 0)
    rows = [
        (lse[0:1], jnp.sum(dd[:64], axis=0, keepdims=True), lane0),
        (lse[64:65], jnp.sum(dd[64:], axis=0, keepdims=True), ~lane0),
    ]
    dq = [None, None]
    for c in range(0, ROWS, B2C):
        k = k_ref[c : c + B2C]
        v = v_ref[c : c + B2C]
        mask = mask_all[c : c + B2C]
        res = []
        for h, (top, inner, pick) in enumerate(rows):
            kh = jnp.where(pick, k, jnp.zeros_like(k))
            vh = jnp.where(pick, v, jnp.zeros_like(v))
            p = jnp.exp(mm_nt(kh, q) + mask - top)
            ds = (p * (mm_nt(vh, do) - inner)).astype(BF)
            res.append((mm(ds, q), mm(p.astype(BF), do)))
            t = mm_tn(ds, k)
            dq[h] = t if c == 0 else dq[h] + t
        dk_ref[c : c + B2C] = jnp.where(lane0, res[0][0], res[1][0]).astype(BF)
        dv_ref[c : c + B2C] = jnp.where(lane0, res[0][1], res[1][1]).astype(BF)
    dq_ref[...] = (jnp.where(lane0, dq[0], dq[1]) * 0.125).astype(BF)


def b2(meta, qkv, do, o, lse, first):
    return call(
        b2_kernel,
        meta,
        (3,),
        [(head_block(first + i), qkv) for i in (0, 6, 12)]
        + [(head_block(first), do), (head_block(first), o), (head_block(first), lse)],
        [(head_block(0), sds((ROWS, D // 2), BF))] * 3,
        us=9,
    )


ERF_TOP = (0.00022905065861350646, 0.0034082910107109506, 0.050955695062380861)
ERF_TOP += (0.18520832239976145, 1.128379143519084)
ERF_LOW = (-1.1791602954361697e-7, 0.000023547966471313185, 0.0010179625278914885)
ERF_LOW += (0.014070470171167667, 0.11098505178285362, 0.49746925110067538, 1.0)


def erf(x):
    x = jnp.clip(x, -3.832506856900711, 3.832506856900711)
    y = x * x
    top = y * ERF_TOP[0] + ERF_TOP[1]
    for a in ERF_TOP[2:]:
        top = top * y + a
    low = y * ERF_LOW[0] + ERF_LOW[1]
    for b in ERF_LOW[2:]:
        low = low * y + b
    r = pl.reciprocal(low, approx=True)
    r = r * (2.0 - low * r)
    return x * top * r


def ff_kernel(
    meta, x_ref, att_ref, gm_in, gg_in, vec_ref, ub_ref, wm0, wm1, wm2, wm3, wm4, wo0, wo1, wo2, wo3, wo4,
    keep_ref, send_ref, gm_ref, ga_ref, grad_m, grad_o, sums_ref, dub_ref,
    mid, inv, n2, act, gh, acc, e2, g_low, w_out, w_buf, g_buf, o_buf, w_sem, g_sem, o_sem,
):
    j = pl.program_id(0)
    core = meta[0]

    def each(count, body):
        lax.fori_loop(0, count, lambda k, _: (body(k), 0)[1], 0)

    def rows(k):
        return pl.ds(pl.multiple_of(k * FFC, FFC), FFC)

    pieces = (((wm0, wm1, wm2, wm3, wm4), core, meta[3]), ((wo0, wo1, wo2, wo3, wo4), 1 - core, meta[4]))

    def fetch(block, act_on):
        slot = block % 2

        def copy_all(parts, at, half):
            own, after, far_low, far_high, before = parts
            for k, src in enumerate((own.at[half], after.at[half], (far_low, far_high)[half], before.at[half])):
                act_on(
                    pltpu.make_async_copy(
                        src.at[:, : 2 * D], w_buf.at[half, (at + k) % 4], w_sem.at[half, k]
                    )
                )

        for parts, owner, at in pieces:
            for half in range(2):
                here = ((block // 2) == owner) & (slot == half)
                pl.when(here)(functools.partial(copy_all, parts, at, half))

    def flush(block, act_on):
        slot = block % 2
        for refs, mine in ((grad_m, True), (grad_o, False)):
            copy = pltpu.make_async_copy(
                g_buf.at[slot], refs.at[:, slot, :, : 2 * D], g_sem.at[slot]
            )
            pl.when(((block // 2) == core) == mine)(lambda: act_on(copy))

    start = lambda copy: copy.start()
    wait = lambda copy: copy.wait()
    out_in = []
    for k, (parts, owner, at) in enumerate(pieces):
        own, after, far_low, far_high, before = parts
        moves = [(own, 0, None), (after, 1, None), (far_low, 2, 0), (far_high, 2, 1), (before, 3, None)]
        for q, (src, step, half) in enumerate(moves):
            dst = o_buf.at[owner, (at + step) % 4]
            src = src.at[:, 2 * D :] if half is not None else src.at[:, :, 2 * D :]
            dst = dst if half is None else dst.at[half]
            out_in.append(pltpu.make_async_copy(src, dst, o_sem.at[5 * k + q]))
    out_back = [
        pltpu.make_async_copy(o_buf.at[place], refs.at[:, :, :, 2 * D :], o_sem.at[k])
        for k, (refs, place) in enumerate(((grad_m, core), (grad_o, 1 - core)))
    ]

    @pl.when(j == 0)
    def _():
        for copy in out_in:
            copy.start()
        fetch(j, start)
        fill(g_low, gm_in[meta[1], 0], gg_in[...])
        acc[...] = jnp.zeros_like(acc)
        e2[...] = jnp.zeros_like(e2)
        for copy in out_in:
            copy.wait()
        for i in range(4):
            w_out[:, 192 * i : 192 * i + 192] = o_buf[i // 2, :, i % 2, :, :192].reshape(D, 192)

        def body(k):
            r = rows(k)
            m = x_ref[r].astype(F32) + (mm(att_ref[r], w_out[...]) + vec_ref[4:5])
            mid[r] = m
            u, i = unit(m)
            inv[r] = jnp.broadcast_to(i, (FFC, 128))
            n2[r] = (u * vec_ref[5:6] + vec_ref[6:7]).astype(BF)

        each(ROWS // FFC, body)

    @pl.when(j < 4)
    def _():
        slot = j % 2
        fetch(j, wait)
        pl.when(j < 3)(lambda: fetch(j + 1, start))
        pl.when(j >= 2)(lambda: flush(j - 2, wait))
        dub_ref[j] = jnp.zeros((1, D), F32)

        def body(k):
            r = rows(k)
            for c in range(0, D, SUB):
                cols = slice(c, c + SUB)
                up = w_buf[slot, :, :, cols].reshape(D, SUB)
                down = w_buf[slot, c // 192 : (c + SUB) // 192, :, D:].reshape(SUB, D)
                h = mm(n2[r], up) + ub_ref[j, :, cols]
                t = mm_nt(g_low[r], down)
                phi = 0.5 + 0.5 * erf(h * math.sqrt(0.5))
                act[r, cols] = (h * phi).astype(BF)
                slope = phi + h * (jnp.exp(h * h * -0.5) * (1.0 / math.sqrt(2.0 * math.pi)))
                t = (t * slope).astype(BF)
                gh[r, cols] = t
                dub_ref[j, :, cols] += jnp.sum(t.astype(F32), axis=0, keepdims=True)
            acc[r] += mm(act[r], w_buf[slot, :, :, D:].reshape(D, D))
            e2[r] += mm_nt(gh[r], w_buf[slot, :, :, :D].reshape(D, D))

        each(ROWS // FFC, body)

        def grads(k):
            c = pl.multiple_of(k * SUB, SUB)
            t = mm_tn(act[:, pl.ds(c, SUB)], g_low[...]).astype(BF)
            g_buf[slot, pl.ds(k * (SUB // 192), SUB // 192), :, D:] = t.reshape(-1, 192, D)
            t = mm_tn(n2[...], gh[:, pl.ds(c, SUB)]).astype(BF)
            g_buf[slot, :, :, pl.ds(c, SUB)] = t.reshape(4, 192, SUB)

        each(D // SUB, grads)
        flush(j, start)

    @pl.when(j == 4)
    def _():
        flush(j - 2, wait)
        sums_ref[...] = jnp.zeros_like(sums_ref)

        def body(k):
            r = rows(k)
            m = mid[r]
            res = (m + (acc[r] + vec_ref[7:8])).astype(BF)
            keep_ref[...] = res[:TOK]
            send_ref[...] = res[HALF : HALF + TOK]
            g = g_low[r].astype(F32)
            e = e2[r]
            i = inv[r][:, 0:1]
            u = (m - jnp.mean(m, axis=-1, keepdims=True)) * i
            grad = g + norm_back(e, u, i, vec_ref[5:6])
            gm_ref[r] = grad
            low = grad.astype(BF)
            n2[r] = low
            ga_ref[r] = mm_nt(low, w_out[...]).astype(BF)
            for q, t in enumerate((low.astype(F32), e * u, e, g)):
                sums_ref[q : q + 1] += jnp.sum(t, axis=0, keepdims=True)

        each(ROWS // FFC, body)
        grad_out = mm_tn(att_ref[...], n2[...]).astype(BF)
        for i in range(4):
            part = grad_out[:, 192 * i : 192 * i + 192].reshape(4, 192, 192)
            o_buf[i // 2, :, i % 2, :, :192] = part
            o_buf[i // 2, :, i % 2, :, 192:] = jnp.zeros((4, 192, 64), BF)
        for copy in out_back:
            copy.start()
        flush(j - 1, wait)
        for copy in out_back:
            copy.wait()


def ff(meta, x, att, cot, cot_got, mine, other, vec, up_bias):
    any_ref = pl.BlockSpec(memory_space=pl.ANY)
    wide = (any_ref, sds((4, 2, 192, 1792), BF))
    half = (whole((TOK, D)), sds((TOK, D), BF))
    ins = [(FULL, x), (FULL, att), (whole((2, 1, TOK, D)), cot), (whole((TOK, D)), cot_got)]
    ins += [(whole((16, D)), vec), (whole((4, 1, D)), up_bias)]
    ins += [(any_ref, piece) for piece in (*mine, *other)]
    outs = [half, half, (FULL, sds((ROWS, D), F32)), (FULL, sds((ROWS, D), BF)), wide, wide]
    outs += [(whole((8, D)), sds((8, D), F32)), (whole((4, 1, D)), sds((4, 1, D), F32))]
    return call(
        ff_kernel,
        meta,
        (5,),
        ins,
        outs,
        [pltpu.VMEM((ROWS, D), F32), pltpu.VMEM((ROWS, 128), F32), pltpu.VMEM((ROWS, D), BF)]
        + [pltpu.VMEM((ROWS, D), BF)] * 2
        + [pltpu.VMEM((ROWS, D), F32)] * 2
        + [pltpu.VMEM((ROWS, D), BF), pltpu.VMEM((D, D), BF)]
        + [pltpu.VMEM((2, 4, 192, 2 * D), BF)] * 2
        + [pltpu.VMEM((2, 4, 2, 192, 256), BF)]
        + [pltpu.SemaphoreType.DMA((2, 4)), pltpu.SemaphoreType.DMA((2,)), pltpu.SemaphoreType.DMA((10,))],
        us=36,
        vmem=VFF,
    )


def b1_kernel(
    meta, x_ref, n1_ref, gm_ref, qa_ref, ka_ref, va_ref, qb_ref, kb_ref, vb_ref, wm_ref, wo_ref, vec_ref, small_ref,
    keep_ref, send_ref, gwm_ref, gwo_ref, gj, e1,
):
    j = pl.program_id(0)
    core = meta[0]

    @pl.when(j == 0)
    def _():
        gj[0, :, 0:384] = qa_ref[...]
        gj[0, :, 384:640] = qb_ref[:, 0:256]
        gj[1, :, 0:128] = qb_ref[:, 256:384]
        gj[1, :, 128:512] = ka_ref[...]
        gj[1, :, 512:640] = kb_ref[:, 0:128]
        gj[2, :, 0:256] = kb_ref[:, 128:384]
        gj[2, :, 256:640] = va_ref[...]
        gj[3, :, 0:384] = vb_ref[...]
        gj[3, :, 384:640] = jnp.zeros((ROWS, 256), BF)
        e1[...] = jnp.zeros_like(e1)

    b = gj[j]

    def block(w_ref, grad_ref):
        e1[...] += mm_nt(b, rows_of(w_ref))
        grad_ref[:, 0] = mm_tn(n1_ref[...], b).astype(BF).reshape(4, 192, 640)

    own = (j // 2) == core
    pl.when(own)(lambda: block(wm_ref, gwm_ref))
    pl.when(jnp.logical_not(own))(lambda: block(wo_ref, gwo_ref))

    @pl.when(j == 3)
    def _():
        tot = [None] * 4
        for c in range(2):
            r = slice(c * HALF, (c + 1) * HALF)
            u, i = unit(x_ref[r].astype(F32))
            e = e1[r]
            grad = gm_ref[r] + norm_back(e, u, i, vec_ref[0:1])
            if c == 0:
                keep_ref[...] = grad[:TOK]
            else:
                send_ref[...] = grad[:TOK].astype(BF)
            sides = [
                jnp.concatenate([left[r], right[r]], axis=1).astype(F32)
                for left, right in ((qa_ref, qb_ref), (va_ref, vb_ref))
            ]
            for k, t in enumerate((e * u, e, *sides)):
                t = jnp.sum(t, axis=0, keepdims=True)
                tot[k] = t if c == 0 else tot[k] + t
        rows = jnp.concatenate(tot + [small_ref[4:16], jnp.zeros((112, D), F32)], axis=0)
        cols = rows.T.astype(BF)

        def put(ref):
            ref[:, 0, :, 384:512] = cols.reshape(4, 192, 128)

        pl.when(core == 1)(lambda: put(gwm_ref))
        pl.when(core == 0)(lambda: put(gwo_ref))


def b1(meta, x, n1, gm, low, high, mine, other, vec, small):
    pair = [(spec(640), sds((4, 2, 192, 640), BF)) for spec in (mine_spec, other_spec)]
    return call(
        b1_kernel,
        meta,
        (4,),
        [(FULL, x), (FULL, n1), (FULL, gm)]
        + [(whole((ROWS, D // 2)), part) for part in (*low, *high)]
        + [(mine_spec(640), mine), (other_spec(640), other), (whole((16, D)), vec), (whole((16, D)), small)],
        [(whole((TOK, D)), sds((TOK, D), F32)), (whole((TOK, D)), sds((TOK, D), BF))] + pair,
        [pltpu.VMEM((4, ROWS, 640), BF), pltpu.VMEM((ROWS, D), F32)],
        us=12,
    )


def ring_groups(axis_zero, axis_one):
    groups = []
    for core, axis in ((0, axis_zero), (1, axis_one)):
        others = [name for name in "zxy" if name != axis]
        for i in range(4):
            for j in range(4):
                at = {others[0]: i, others[1]: j}
                line = []
                for k in range(4):
                    at[axis] = k
                    z, x, y = at["z"], at["x"], at["y"]
                    line.append((((z * 2 + x // 2) * 4 + y) * 2 + core) * 2 + x % 2)
                groups.append(line)
    return groups


ZY = ring_groups("z", "y")
YZ = ring_groups("y", "z")


def swap(value, axis):
    return lax.ppermute(value, axis, [(0, 1), (1, 0)])


def tie(*values):
    return lax.optimization_barrier(values)


CROSS = [(4 * i + k, 4 * k + i) for i in range(4) for k in range(4)]


def cross(value):
    return lax.ppermute(value, ("z", "y"), CROSS)


def along(value, groups):
    return lax.all_to_all(value, AXES, 0, 0, tiled=True, axis_index_groups=groups)


def copies(value, groups):
    return along(jnp.broadcast_to(value[None], (4, *value.shape)), groups)


def step_along(value, groups, step):
    pairs = [(line[i], line[(i + step) % 4]) for line in groups for i in range(4)]
    return lax.ppermute(value, AXES, pairs)


def among(value):
    return lax.all_to_all(value, ("core", "xh", "xl"), 0, 0, tiled=True)


def per_device(
    inputs,
    cotangent,
    lengths,
    w_qkv,
    w_out,
    w_up,
    w_down,
    ln1_gain,
    ln1_shift,
    q_bias,
    v_bias,
    out_bias,
    ln2_gain,
    ln2_shift,
    up_bias,
    down_bias,
):
    side = lax.axis_index("xl")
    core = lax.axis_index("core")

    def theirs(block):
        return swap(lax.dynamic_index_in_dim(block, 1 - side, 0, keepdims=False)[0], "xl")

    def give_back(kept, got):
        got = got.astype(kept.dtype)
        first = side == 0
        return jnp.stack([jnp.where(first, kept, got), jnp.where(first, got, kept)])[:, None]

    got_image = theirs(inputs)

    row = lax.broadcasted_iota(jnp.int32, (12, 6), 0)
    smalls = jnp.pad(up_bias.reshape(4, 6), ((8, 0), (0, 0)))
    for i, part in enumerate(
        (ln1_gain, ln1_shift, q_bias, v_bias, out_bias, ln2_gain, ln2_shift, down_bias)
    ):
        smalls = jnp.where(row == i, part[None], smalls)
    wide_one = jnp.concatenate([w_qkv, smalls.T, jnp.zeros((6, 244), BF)], axis=1)
    cut_out = jnp.pad(w_out.reshape(6, 4, 192), ((0, 0), (0, 0), (0, 64)))
    cut_up = w_up.reshape(6, 32, 4, 24).transpose(0, 2, 1, 3).reshape(6, 4, D)
    cut = jnp.concatenate([wide_one.reshape(6, 4, 640), cut_up, cut_out], axis=2)
    cut = jnp.moveaxis(cut, 1, 0).reshape(2, 12, 1664)
    cut = jnp.concatenate([cut, jnp.stack([w_down.reshape(12, 2 * D)] * 2)], axis=2)
    sent = jnp.stack([cut[0]] * 4 + [cross(cut[1])] * 4)
    line = among(sent)
    blocks = line[..., :1664].reshape(2, 2, 2, 2, 6, 1664).transpose(3, 1, 0, 2, 4, 5)
    downs = lax.dynamic_index_in_dim(line.reshape(2, 2, 2, 12, 3200), core, 0, keepdims=False)
    downs = downs[..., 1664:].reshape(2, 2, 24, D).transpose(1, 0, 2, 3)
    blocks = blocks.reshape(2, 2, 24, 1664)
    line = jnp.concatenate([blocks[..., :1408], downs, blocks[..., 1408:]], axis=3)
    plane = copies(line, YZ).transpose(1, 2, 0, 3, 4).reshape(384, 2432)
    plane, got_image = tie(plane, got_image)
    one_mine = copies(plane[:, :640], ZY).reshape(4, 2, 192, 640)
    own = plane[:, 640:].reshape(2, 192, 1792)
    own, one_mine = tie(own, one_mine)
    one_other = swap(one_mine, "core")
    before, after = step_along(own, ZY, 1), step_along(own, ZY, 3)

    got_cotangent = theirs(cotangent)
    length = lax.dynamic_index_in_dim(lengths, side, 0, keepdims=False)[0]
    z, y = lax.axis_index("z"), lax.axis_index("y")
    at_mine, at_other = jnp.where(core == 0, z, y), jnp.where(core == 0, y, z)
    meta = jnp.stack([core, side, length, at_mine, at_other]).astype(jnp.int32)

    qkv, normed, vecs, image = f1(meta, inputs, got_image, one_mine, one_other)
    before, after, qkv, got_cotangent = tie(before, after, qkv, got_cotangent)
    far_low, far_high = step_along(before[0], ZY, 1), step_along(after[1], ZY, 3)
    near = [swap(part, "core") for part in (own, after, before)]
    attended, log_total = f2(meta, qkv)
    far_low, far_high, attended, *near = tie(far_low, far_high, attended, *near)
    mine = (own, after, far_low, far_high, before)
    other = (near[0], near[1], swap(far_low, "core"), swap(far_high, "core"), near[2])
    up_order = vecs[8:12].reshape(4, 32, 4, 6).transpose(2, 1, 0, 3).reshape(4, 1, D)

    attended, up_order = tie(attended, up_order)
    (
        kept_result,
        sent_result,
        grad_middle,
        grad_attended,
        wide_kept,
        wide_away,
        sums,
        up_sums,
    ) = ff(
        meta,
        image,
        attended,
        cotangent,
        got_cotangent,
        mine,
        other,
        vecs,
        up_order,
    )

    got_wide = swap(wide_away, "core")
    low = b2(meta, qkv, grad_attended, attended, log_total, 0)
    got_wide, *low = tie(got_wide, *low)
    two = (wide_kept.astype(F32) + got_wide.astype(F32)).astype(BF)
    two, grad_attended = tie(two, grad_attended)
    two = along(two, ZY)

    high = b2(meta, qkv, grad_attended, attended, log_total, 3)
    sent_result, up_sums, sums, *high = tie(sent_result, up_sums, sums, *high)
    got_result = swap(sent_result, "xl")
    up_sums = up_sums.reshape(4, 32, 4, 6).transpose(2, 1, 0, 3).reshape(4, D)
    small_sums = jnp.concatenate(
        [jnp.zeros((4, D), F32), sums[:4], up_sums, jnp.zeros((4, D), F32)]
    )
    kept_grad, sent_grad, one_kept, one_away = b1(
        meta, image, normed, grad_middle, low, high, one_mine, one_other, vecs, small_sums
    )
    one_kept, one_away, got_result = tie(one_kept, one_away, got_result)
    one = (one_kept.astype(F32) + swap(one_away, "core").astype(F32)).astype(BF)
    one, two = tie(one, two)
    one = along(one, ZY)

    def shrink(parts):
        return jnp.sum(parts.astype(F32), axis=0).astype(BF)

    def plane_of(parts):
        return shrink(parts).reshape(2, 2, 4, 24, parts.shape[-1]).transpose(2, 0, 1, 3, 4)

    two = plane_of(two)
    place = at_other

    def piece(step):
        part = lax.dynamic_index_in_dim(two, (place + step) % 4, 0, keepdims=False)
        if step:
            part = step_along(part, YZ, step)
        return part.astype(F32)

    two = (piece(0) + piece(1) + piece(2) + piece(3)).astype(BF)
    one = shrink(along(plane_of(one), YZ))
    line = jnp.concatenate([one, two], axis=3)
    blocks = jnp.concatenate([line[..., :1408], line[..., 2176:]], axis=3)
    blocks = blocks.reshape(2, 2, 2, 2, 6, 1664).transpose(2, 1, 3, 0, 4, 5).reshape(8, 12, 1664)
    downs = line[..., 1408:2176].transpose(1, 0, 2, 3).reshape(1, 4, 12, 2 * D)
    downs = jnp.concatenate([downs, downs]).reshape(8, 12, 2 * D)
    got = among(jnp.concatenate([blocks, downs], axis=2)).reshape(2, 4, 12, 3200)
    got = jnp.sum(got.astype(F32), axis=1)
    high = cross(got[1].astype(BF)).astype(F32)
    own_down = jnp.where(core == 0, got[0, :, 1664:], high[:, 1664:]).reshape(24, D)
    back = jnp.stack([got[0, :, :1664], high[:, :1664]]).reshape(4, 6, 1664)
    own_one = jnp.moveaxis(back[..., :640], 0, 1).reshape(6, 2560)
    own_up = back[..., 640:1408].reshape(4, 6, 32, 24).transpose(1, 2, 0, 3).reshape(6, FF)
    own_out = jnp.moveaxis(back[..., 1408:1600], 0, 1).reshape(6, D)
    small = own_one[:, 3 * D : 3 * D + 12].T
    return (
        give_back(kept_result, got_result),
        give_back(kept_grad, swap(sent_grad, "xl")),
        own_one[:, : 3 * D],
        own_out,
        own_up,
        own_down,
        small[0],
        small[1],
        small[2],
        small[3],
        small[4],
        small[5],
        small[6],
        small[8:].reshape(24),
        small[7],
    )


def solution(mesh):
    fine = Mesh(mesh.devices.reshape(4, 2, 4, 2, 2), AXES)
    images = ("z", "xh", "y", "core")
    rows, vec = P(AXES, None), P(AXES)
    tokens = P(None, images, "xl", None)
    return jax.shard_map(
        per_device,
        mesh=fine,
        in_specs=(tokens, tokens, P(None, images)) + (rows,) * 4 + (vec,) * 9,
        out_specs=(tokens, tokens) + (rows,) * 4 + (vec,) * 9,
        check_vma=False,
    )
```

```python
import functools
import math

import jax
import jax.numpy as jnp
from jax import lax
from jax.experimental import pallas as pl
from jax.experimental.pallas import tpu as pltpu
from jax.sharding import Mesh
from jax.sharding import PartitionSpec as P

D = 768
FF = 3072
TOK = 290
HALF = 320
ROWS = 2 * HALF
AXES = ("z", "xh", "y", "core", "xl")
BF = jnp.bfloat16
F32 = jnp.float32
F2C = 640
B2C = 640
SUB = 768
FFC = 640
VFF = 60


def mm(a, b):
    return lax.dot_general(a, b, (((1,), (0,)), ((), ())), preferred_element_type=F32)


def mm_nt(a, b):
    return lax.dot_general(a, b, (((1,), (1,)), ((), ())), preferred_element_type=F32)


def mm_tn(a, b):
    return lax.dot_general(a, b, (((0,), (0,)), ((), ())), preferred_element_type=F32)


def unit(values):
    centred = values - jnp.mean(values, axis=-1, keepdims=True)
    inverse = lax.rsqrt(jnp.mean(centred * centred, axis=-1, keepdims=True) + 1e-06)
    return centred * inverse, inverse


def norm_back(e, u, inverse, gain):
    s = e * gain
    mean = jnp.mean(s, axis=-1, keepdims=True)
    return inverse * (s - mean - u * jnp.mean(s * u, axis=-1, keepdims=True))


def call(kernel, meta, grid, ins, outs, scratch=(), us=10, vmem=60):
    return pl.pallas_call(
        kernel,
        grid_spec=pltpu.PrefetchScalarGridSpec(
            num_scalar_prefetch=1,
            grid=grid,
            in_specs=[spec for spec, _ in ins],
            out_specs=[spec for spec, _ in outs],
            scratch_shapes=list(scratch),
        ),
        out_shape=[shape for _, shape in outs],
        cost_estimate=pl.CostEstimate(
            flops=us * 10**9, bytes_accessed=us * 3 * 10**6, transcendentals=0
        ),
        compiler_params=pltpu.CompilerParams(vmem_limit_bytes=vmem * 2**20),
    )(meta, *[array for _, array in ins])


def whole(shape):
    return pl.BlockSpec(shape, lambda *_: (0,) * len(shape))


def sds(shape, dt):
    return jax.ShapeDtypeStruct(shape, dt)


def mine_spec(n):
    return pl.BlockSpec((4, 1, 192, n), lambda j, m: (0, jnp.clip(j - 2 * m[0], 0, 1), 0, 0))


def other_spec(n):
    return pl.BlockSpec((4, 1, 192, n), lambda j, m: (0, jnp.clip(j - 2 + 2 * m[0], 0, 1), 0, 0))


def rows_of(ref, i=0):
    return ref[:, i].reshape(D, ref.shape[-1])


OWN_HALF = pl.BlockSpec((1, 1, TOK, D), lambda j, m: (m[1], 0, 0, 0))
FULL = whole((ROWS, D))


def fill(ref, mine, got):
    ref[0:TOK] = mine
    ref[TOK:HALF] = jnp.zeros((HALF - TOK, D), BF)
    ref[HALF : HALF + TOK] = got
    ref[HALF + TOK :] = jnp.zeros((HALF - TOK, D), BF)


def key_ok(meta, shape, axis):
    slot = lax.broadcasted_iota(jnp.int32, shape, axis)
    half = (slot >= HALF).astype(jnp.int32)
    within = slot - half * HALF
    half = jnp.where(meta[1] == 1, 1 - half, half)
    return jnp.where((within < TOK) & (within + TOK * half < meta[2]), 0.0, -1e30).astype(F32)


def f1_kernel(meta, x_ref, got_ref, sm_ref, so_ref, wm_ref, wo_ref, qkv_ref, n1_ref, vec_ref, im_ref, bias_ref):
    j = pl.program_id(0)

    @pl.when(j == 0)
    def _():
        small = jnp.where(meta[0] == 1, rows_of(sm_ref).astype(F32), rows_of(so_ref).astype(F32))
        vec = small.T[:16]
        vec_ref[...] = vec
        fill(im_ref, x_ref[0, 0], got_ref[...])
        u, _ = unit(im_ref[...].astype(F32))
        n1_ref[...] = (u * vec[0:1] + vec[1:2]).astype(BF)
        bias_ref[...] = jnp.zeros_like(bias_ref)
        bias_ref[0:1, 0:D] = vec[2:3]
        bias_ref[0:1, 2 * D : 3 * D] = vec[3:4]

    b = bias_ref[0:1, pl.ds(pl.multiple_of(j * 640, 128), 640)]
    own = (j // 2) == meta[0]

    @pl.when(own)
    def _():
        qkv_ref[...] = (mm(n1_ref[...], rows_of(wm_ref)) + b).astype(BF)

    @pl.when(jnp.logical_not(own))
    def _():
        qkv_ref[...] = (mm(n1_ref[...], rows_of(wo_ref)) + b).astype(BF)


def f1(meta, x, got, mine, other):
    tail = pl.BlockSpec((4, 1, 192, 128), lambda j, m: (0, 1, 0, 3))
    return call(
        f1_kernel,
        meta,
        (4,),
        [(OWN_HALF, x), (whole((TOK, D)), got), (tail, mine), (tail, other)]
        + [(mine_spec(640), mine), (other_spec(640), other)],
        [
            (pl.BlockSpec((ROWS, 640), lambda j, m: (0, j)), sds((ROWS, 2560), BF)),
            (FULL, sds((ROWS, D), BF)),
            (whole((16, D)), sds((16, D), F32)),
            (FULL, sds((ROWS, D), BF)),
        ],
        [pltpu.VMEM((8, 2560), F32)],
        us=6,
        vmem=24,
    )


def head_block(first):
    return pl.BlockSpec((ROWS, 128), lambda h, m: (0, h + first))


def f2_kernel(meta, q_ref, k_ref, v_ref, o_ref, lse_ref):
    lane0 = lax.broadcasted_iota(jnp.int32, (1, 128), 1) < 64
    k = k_ref[...]
    v = v_ref[...]
    mask = key_ok(meta, (1, ROWS), 1)
    for c in range(0, ROWS, F2C):
        q = q_ref[c : c + F2C] * jnp.asarray(0.125, BF)
        res = []
        for pick in (lane0, ~lane0):
            s = mm_nt(jnp.where(pick, q, jnp.zeros_like(q)), k) + mask
            top = jnp.max(s, axis=-1, keepdims=True)
            p = jnp.exp(s - top)
            total = jnp.sum(p, axis=-1, keepdims=True)
            o = mm(p.astype(BF), v) * (1.0 / total)
            res.append((o, jnp.broadcast_to(top + jnp.log(total), (F2C, 128))))
        o_ref[c : c + F2C] = jnp.where(lane0, res[0][0], res[1][0]).astype(BF)
        lse_ref[c : c + F2C] = jnp.where(lane0, res[0][1], res[1][1])


def f2(meta, qkv, first):
    return call(
        f2_kernel,
        meta,
        (3,),
        [(head_block(first + i), qkv) for i in (0, 6, 12)],
        [(head_block(0), sds((ROWS, D // 2), BF)), (head_block(0), sds((ROWS, D // 2), F32))],
        us=6,
        vmem=24,
    )


def b2_kernel(meta, q_ref, k_ref, v_ref, do_ref, o_ref, lse_ref, dq_ref, dk_ref, dv_ref):
    lane0 = lax.broadcasted_iota(jnp.int32, (1, 128), 1) < 64
    q = q_ref[...] * jnp.asarray(0.125, BF)
    do = do_ref[...]
    lse = lse_ref[...].T
    dd = (do.astype(F32) * o_ref[...].astype(F32)).T
    mask_all = key_ok(meta, (ROWS, 1), 0)
    rows = [
        (lse[0:1], jnp.sum(dd[:64], axis=0, keepdims=True), lane0),
        (lse[64:65], jnp.sum(dd[64:], axis=0, keepdims=True), ~lane0),
    ]
    dq = [None, None]
    for c in range(0, ROWS, B2C):
        k = k_ref[c : c + B2C]
        v = v_ref[c : c + B2C]
        mask = mask_all[c : c + B2C]
        res = []
        for h, (top, inner, pick) in enumerate(rows):
            kh = jnp.where(pick, k, jnp.zeros_like(k))
            vh = jnp.where(pick, v, jnp.zeros_like(v))
            p = jnp.exp(mm_nt(kh, q) + mask - top)
            ds = (p * (mm_nt(vh, do) - inner)).astype(BF)
            res.append((mm(ds, q), mm(p.astype(BF), do)))
            t = mm_tn(ds, k)
            dq[h] = t if c == 0 else dq[h] + t
        dk_ref[c : c + B2C] = jnp.where(lane0, res[0][0], res[1][0]).astype(BF)
        dv_ref[c : c + B2C] = jnp.where(lane0, res[0][1], res[1][1]).astype(BF)
    dq_ref[...] = (jnp.where(lane0, dq[0], dq[1]) * 0.125).astype(BF)


def b2(meta, qkv, do, o, lse, first):
    return call(
        b2_kernel,
        meta,
        (3,),
        [(head_block(first + i), qkv) for i in (0, 6, 12)]
        + [(head_block(first), do), (head_block(0), o), (head_block(0), lse)],
        [(head_block(0), sds((ROWS, D // 2), BF))] * 3,
        us=9,
    )


ERF_TOP = (0.00022905065861350646, 0.0034082910107109506, 0.050955695062380861)
ERF_TOP += (0.18520832239976145, 1.128379143519084)
ERF_LOW = (-1.1791602954361697e-7, 0.000023547966471313185, 0.0010179625278914885)
ERF_LOW += (0.014070470171167667, 0.11098505178285362, 0.49746925110067538, 1.0)


def erf(x):
    x = jnp.clip(x, -3.832506856900711, 3.832506856900711)
    y = x * x
    top = y * ERF_TOP[0] + ERF_TOP[1]
    for a in ERF_TOP[2:]:
        top = top * y + a
    low = y * ERF_LOW[0] + ERF_LOW[1]
    for b in ERF_LOW[2:]:
        low = low * y + b
    r = pl.reciprocal(low, approx=True)
    r = r * (2.0 - low * r)
    return x * top * r


def ff_kernel(
    meta, x_ref, att_a, att_b, gm_in, gg_in, vec_ref, ub_ref, wm0, wm1, wm2, wm3, wm4, wo0, wo1, wo2, wo3, wo4,
    keep_ref, send_ref, gm_ref, ga_ref, grad_m, grad_o, sums_ref, dub_ref,
    mid, inv, n2, act, gh, acc, e2, g_low, w_out, w_buf, g_buf, o_buf, w_sem, g_sem, o_sem,
):
    j = pl.program_id(0)
    core = meta[0]

    def each(count, body):
        lax.fori_loop(0, count, lambda k, _: (body(k), 0)[1], 0)

    def rows(k):
        return pl.ds(pl.multiple_of(k * FFC, FFC), FFC)

    pieces = (((wm0, wm1, wm2, wm3, wm4), core, meta[3]), ((wo0, wo1, wo2, wo3, wo4), 1 - core, meta[4]))

    def fetch(block, act_on):
        slot = block % 2

        def copy_all(parts, at, half):
            own, after, far_low, far_high, before = parts
            for k, src in enumerate((own.at[half], after.at[half], (far_low, far_high)[half], before.at[half])):
                act_on(
                    pltpu.make_async_copy(
                        src.at[:, : 2 * D], w_buf.at[half, (at + k) % 4], w_sem.at[half, k]
                    )
                )

        for parts, owner, at in pieces:
            for half in range(2):
                here = ((block // 2) == owner) & (slot == half)
                pl.when(here)(functools.partial(copy_all, parts, at, half))

    def flush(block, act_on):
        slot = block % 2
        for refs, mine in ((grad_m, True), (grad_o, False)):
            copy = pltpu.make_async_copy(
                g_buf.at[slot], refs.at[:, slot, :, : 2 * D], g_sem.at[slot]
            )
            pl.when(((block // 2) == core) == mine)(lambda: act_on(copy))

    start = lambda copy: copy.start()
    wait = lambda copy: copy.wait()
    out_in = []
    for k, (parts, owner, at) in enumerate(pieces):
        own, after, far_low, far_high, before = parts
        moves = [(own, 0, None), (after, 1, None), (far_low, 2, 0), (far_high, 2, 1), (before, 3, None)]
        for q, (src, step, half) in enumerate(moves):
            dst = o_buf.at[owner, (at + step) % 4]
            src = src.at[:, 2 * D :] if half is not None else src.at[:, :, 2 * D :]
            dst = dst if half is None else dst.at[half]
            out_in.append(pltpu.make_async_copy(src, dst, o_sem.at[5 * k + q]))
    out_back = [
        pltpu.make_async_copy(o_buf.at[place], refs.at[:, :, :, 2 * D :], o_sem.at[k])
        for k, (refs, place) in enumerate(((grad_m, core), (grad_o, 1 - core)))
    ]

    @pl.when(j == 0)
    def _():
        for copy in out_in:
            copy.start()
        fetch(j, start)
        fill(g_low, gm_in[meta[1], 0], gg_in[...])
        acc[...] = jnp.zeros_like(acc)
        e2[...] = jnp.zeros_like(e2)
        for copy in out_in:
            copy.wait()
        for i in range(4):
            w_out[:, 192 * i : 192 * i + 192] = o_buf[i // 2, :, i % 2, :, :192].reshape(D, 192)

        def body(k):
            r = rows(k)
            branch = mm(att_a[r], w_out[: D // 2]) + mm(att_b[r], w_out[D // 2 :])
            m = x_ref[r].astype(F32) + (branch + vec_ref[4:5])
            mid[r] = m
            u, i = unit(m)
            inv[r] = jnp.broadcast_to(i, (FFC, 128))
            n2[r] = (u * vec_ref[5:6] + vec_ref[6:7]).astype(BF)

        each(ROWS // FFC, body)

    @pl.when(j < 4)
    def _():
        slot = j % 2
        fetch(j, wait)
        pl.when(j < 3)(lambda: fetch(j + 1, start))
        pl.when(j >= 2)(lambda: flush(j - 2, wait))
        dub_ref[j] = jnp.zeros((1, D), F32)

        def body(k):
            r = rows(k)
            for c in range(0, D, SUB):
                cols = slice(c, c + SUB)
                up = w_buf[slot, :, :, cols].reshape(D, SUB)
                down = w_buf[slot, c // 192 : (c + SUB) // 192, :, D:].reshape(SUB, D)
                h = mm(n2[r], up) + ub_ref[j, :, cols]
                t = mm_nt(g_low[r], down)
                phi = 0.5 + 0.5 * erf(h * math.sqrt(0.5))
                act[r, cols] = (h * phi).astype(BF)
                slope = phi + h * (jnp.exp(h * h * -0.5) * (1.0 / math.sqrt(2.0 * math.pi)))
                t = (t * slope).astype(BF)
                gh[r, cols] = t
                dub_ref[j, :, cols] += jnp.sum(t.astype(F32), axis=0, keepdims=True)
            acc[r] += mm(act[r], w_buf[slot, :, :, D:].reshape(D, D))
            e2[r] += mm_nt(gh[r], w_buf[slot, :, :, :D].reshape(D, D))

        each(ROWS // FFC, body)

        def grads(k):
            c = pl.multiple_of(k * SUB, SUB)
            t = mm_tn(act[:, pl.ds(c, SUB)], g_low[...]).astype(BF)
            g_buf[slot, pl.ds(k * (SUB // 192), SUB // 192), :, D:] = t.reshape(-1, 192, D)
            t = mm_tn(n2[...], gh[:, pl.ds(c, SUB)]).astype(BF)
            g_buf[slot, :, :, pl.ds(c, SUB)] = t.reshape(4, 192, SUB)

        each(D // SUB, grads)
        flush(j, start)

    @pl.when(j == 4)
    def _():
        flush(j - 2, wait)
        sums_ref[...] = jnp.zeros_like(sums_ref)

        def body(k):
            r = rows(k)
            m = mid[r]
            res = (m + (acc[r] + vec_ref[7:8])).astype(BF)
            keep_ref[...] = res[:TOK]
            send_ref[...] = res[HALF : HALF + TOK]
            g = g_low[r].astype(F32)
            e = e2[r]
            i = inv[r][:, 0:1]
            u = (m - jnp.mean(m, axis=-1, keepdims=True)) * i
            grad = g + norm_back(e, u, i, vec_ref[5:6])
            gm_ref[r] = grad
            low = grad.astype(BF)
            n2[r] = low
            ga_ref[r] = mm_nt(low, w_out[...]).astype(BF)
            for q, t in enumerate((low.astype(F32), e * u, e, g)):
                sums_ref[q : q + 1] += jnp.sum(t, axis=0, keepdims=True)

        each(ROWS // FFC, body)
        grad_out = jnp.concatenate([mm_tn(att[...], n2[...]) for att in (att_a, att_b)])
        grad_out = grad_out.astype(BF)
        for i in range(4):
            part = grad_out[:, 192 * i : 192 * i + 192].reshape(4, 192, 192)
            o_buf[i // 2, :, i % 2, :, :192] = part
            o_buf[i // 2, :, i % 2, :, 192:] = jnp.zeros((4, 192, 64), BF)
        for copy in out_back:
            copy.start()
        flush(j - 1, wait)
        for copy in out_back:
            copy.wait()


def ff(meta, x, att, cot, cot_got, mine, other, vec, up_bias):
    any_ref = pl.BlockSpec(memory_space=pl.ANY)
    wide = (any_ref, sds((4, 2, 192, 1792), BF))
    half = (whole((TOK, D)), sds((TOK, D), BF))
    ins = [(FULL, x)] + [(whole((ROWS, D // 2)), part) for part in att]
    ins += [(whole((2, 1, TOK, D)), cot), (whole((TOK, D)), cot_got)]
    ins += [(whole((16, D)), vec), (whole((4, 1, D)), up_bias)]
    ins += [(any_ref, piece) for piece in (*mine, *other)]
    outs = [half, half, (FULL, sds((ROWS, D), F32)), (FULL, sds((ROWS, D), BF)), wide, wide]
    outs += [(whole((8, D)), sds((8, D), F32)), (whole((4, 1, D)), sds((4, 1, D), F32))]
    return call(
        ff_kernel,
        meta,
        (5,),
        ins,
        outs,
        [pltpu.VMEM((ROWS, D), F32), pltpu.VMEM((ROWS, 128), F32), pltpu.VMEM((ROWS, D), BF)]
        + [pltpu.VMEM((ROWS, D), BF)] * 2
        + [pltpu.VMEM((ROWS, D), F32)] * 2
        + [pltpu.VMEM((ROWS, D), BF), pltpu.VMEM((D, D), BF)]
        + [pltpu.VMEM((2, 4, 192, 2 * D), BF)] * 2
        + [pltpu.VMEM((2, 4, 2, 192, 256), BF)]
        + [pltpu.SemaphoreType.DMA((2, 4)), pltpu.SemaphoreType.DMA((2,)), pltpu.SemaphoreType.DMA((10,))],
        us=36,
        vmem=VFF,
    )


def b1_kernel(
    meta, x_ref, n1_ref, gm_ref, qa_ref, ka_ref, va_ref, qb_ref, kb_ref, vb_ref, wm_ref, wo_ref, vec_ref, small_ref,
    keep_ref, send_ref, gwm_ref, gwo_ref, gj, e1,
):
    j = pl.program_id(0)
    core = meta[0]

    @pl.when(j == 0)
    def _():
        gj[0, :, 0:384] = qa_ref[...]
        gj[0, :, 384:640] = qb_ref[:, 0:256]
        gj[1, :, 0:128] = qb_ref[:, 256:384]
        gj[1, :, 128:512] = ka_ref[...]
        gj[1, :, 512:640] = kb_ref[:, 0:128]
        gj[2, :, 0:256] = kb_ref[:, 128:384]
        gj[2, :, 256:640] = va_ref[...]
        gj[3, :, 0:384] = vb_ref[...]
        gj[3, :, 384:640] = jnp.zeros((ROWS, 256), BF)
        e1[...] = jnp.zeros_like(e1)

    b = gj[j]

    def block(w_ref, grad_ref):
        e1[...] += mm_nt(b, rows_of(w_ref))
        grad_ref[:, 0] = mm_tn(n1_ref[...], b).astype(BF).reshape(4, 192, 640)

    own = (j // 2) == core
    pl.when(own)(lambda: block(wm_ref, gwm_ref))
    pl.when(jnp.logical_not(own))(lambda: block(wo_ref, gwo_ref))

    @pl.when(j == 3)
    def _():
        tot = [None] * 4
        for c in range(2):
            r = slice(c * HALF, (c + 1) * HALF)
            u, i = unit(x_ref[r].astype(F32))
            e = e1[r]
            grad = gm_ref[r] + norm_back(e, u, i, vec_ref[0:1])
            if c == 0:
                keep_ref[...] = grad[:TOK]
            else:
                send_ref[...] = grad[:TOK].astype(BF)
            sides = [
                jnp.concatenate([left[r], right[r]], axis=1).astype(F32)
                for left, right in ((qa_ref, qb_ref), (va_ref, vb_ref))
            ]
            for k, t in enumerate((e * u, e, *sides)):
                t = jnp.sum(t, axis=0, keepdims=True)
                tot[k] = t if c == 0 else tot[k] + t
        rows = jnp.concatenate(tot + [small_ref[4:16], jnp.zeros((112, D), F32)], axis=0)
        cols = rows.T.astype(BF)

        def put(ref):
            ref[:, 0, :, 384:512] = cols.reshape(4, 192, 128)

        pl.when(core == 1)(lambda: put(gwm_ref))
        pl.when(core == 0)(lambda: put(gwo_ref))


def b1(meta, x, n1, gm, low, high, mine, other, vec, small):
    pair = [(spec(640), sds((4, 2, 192, 640), BF)) for spec in (mine_spec, other_spec)]
    return call(
        b1_kernel,
        meta,
        (4,),
        [(FULL, x), (FULL, n1), (FULL, gm)]
        + [(whole((ROWS, D // 2)), part) for part in (*low, *high)]
        + [(mine_spec(640), mine), (other_spec(640), other), (whole((16, D)), vec), (whole((16, D)), small)],
        [(whole((TOK, D)), sds((TOK, D), F32)), (whole((TOK, D)), sds((TOK, D), BF))] + pair,
        [pltpu.VMEM((4, ROWS, 640), BF), pltpu.VMEM((ROWS, D), F32)],
        us=12,
    )


def ring_groups(axis_zero, axis_one):
    groups = []
    for core, axis in ((0, axis_zero), (1, axis_one)):
        others = [name for name in "zxy" if name != axis]
        for i in range(4):
            for j in range(4):
                at = {others[0]: i, others[1]: j}
                line = []
                for k in range(4):
                    at[axis] = k
                    z, x, y = at["z"], at["x"], at["y"]
                    line.append((((z * 2 + x // 2) * 4 + y) * 2 + core) * 2 + x % 2)
                groups.append(line)
    return groups


ZY = ring_groups("z", "y")
YZ = ring_groups("y", "z")


def swap(value, axis):
    return lax.ppermute(value, axis, [(0, 1), (1, 0)])


def tie(*values):
    return lax.optimization_barrier(values)


CROSS = [(4 * i + k, 4 * k + i) for i in range(4) for k in range(4)]


def cross(value):
    return lax.ppermute(value, ("z", "y"), CROSS)


def along(value, groups):
    return lax.all_to_all(value, AXES, 0, 0, tiled=True, axis_index_groups=groups)


def copies(value, groups):
    return along(jnp.broadcast_to(value[None], (4, *value.shape)), groups)


def step_along(value, groups, step):
    pairs = [(line[i], line[(i + step) % 4]) for line in groups for i in range(4)]
    return lax.ppermute(value, AXES, pairs)


def among(value):
    return lax.all_to_all(value, ("core", "xh", "xl"), 0, 0, tiled=True)


def per_device(
    inputs,
    cotangent,
    lengths,
    w_qkv,
    w_out,
    w_up,
    w_down,
    ln1_gain,
    ln1_shift,
    q_bias,
    v_bias,
    out_bias,
    ln2_gain,
    ln2_shift,
    up_bias,
    down_bias,
):
    side = lax.axis_index("xl")
    core = lax.axis_index("core")

    def theirs(block):
        return swap(lax.dynamic_index_in_dim(block, 1 - side, 0, keepdims=False)[0], "xl")

    def give_back(kept, got):
        got = got.astype(kept.dtype)
        first = side == 0
        return jnp.stack([jnp.where(first, kept, got), jnp.where(first, got, kept)])[:, None]

    got_image = theirs(inputs)

    row = lax.broadcasted_iota(jnp.int32, (12, 6), 0)
    smalls = jnp.pad(up_bias.reshape(4, 6), ((8, 0), (0, 0)))
    for i, part in enumerate(
        (ln1_gain, ln1_shift, q_bias, v_bias, out_bias, ln2_gain, ln2_shift, down_bias)
    ):
        smalls = jnp.where(row == i, part[None], smalls)
    wide_one = jnp.concatenate([w_qkv, smalls.T, jnp.zeros((6, 244), BF)], axis=1)
    cut_out = jnp.pad(w_out.reshape(6, 4, 192), ((0, 0), (0, 0), (0, 64)))
    cut_up = w_up.reshape(6, 32, 4, 24).transpose(0, 2, 1, 3).reshape(6, 4, D)
    cut = jnp.concatenate([wide_one.reshape(6, 4, 640), cut_up, cut_out], axis=2)
    cut = jnp.moveaxis(cut, 1, 0).reshape(2, 12, 1664)
    cut = jnp.concatenate([cut, jnp.stack([w_down.reshape(12, 2 * D)] * 2)], axis=2)
    sent = jnp.stack([cut[0]] * 4 + [cross(cut[1])] * 4)
    line = among(sent)
    blocks = line[..., :1664].reshape(2, 2, 2, 2, 6, 1664).transpose(3, 1, 0, 2, 4, 5)
    downs = lax.dynamic_index_in_dim(line.reshape(2, 2, 2, 12, 3200), core, 0, keepdims=False)
    downs = downs[..., 1664:].reshape(2, 2, 24, D).transpose(1, 0, 2, 3)
    blocks = blocks.reshape(2, 2, 24, 1664)
    line = jnp.concatenate([blocks[..., :1408], downs, blocks[..., 1408:]], axis=3)
    plane = copies(line, YZ).transpose(1, 2, 0, 3, 4).reshape(384, 2432)
    plane, got_image = tie(plane, got_image)
    one_mine = copies(plane[:, :640], ZY).reshape(4, 2, 192, 640)
    own = plane[:, 640:].reshape(2, 192, 1792)
    got_cotangent = theirs(cotangent)
    length = lax.dynamic_index_in_dim(lengths, side, 0, keepdims=False)[0]
    z, y = lax.axis_index("z"), lax.axis_index("y")
    at_mine, at_other = jnp.where(core == 0, z, y), jnp.where(core == 0, y, z)
    meta = jnp.stack([core, side, length, at_mine, at_other]).astype(jnp.int32)
    own, one_mine, got_cotangent, meta = tie(own, one_mine, got_cotangent, meta)
    one_other = swap(one_mine, "core")
    before, after = step_along(own, ZY, 1), step_along(own, ZY, 3)

    qkv, normed, vecs, image = f1(meta, inputs, got_image, one_mine, one_other)
    att_low, total_low = f2(meta, qkv, 0)
    before, after, qkv, att_low = tie(before, after, qkv, att_low)
    far_low, far_high = step_along(before[0], ZY, 1), step_along(after[1], ZY, 3)
    near = [swap(part, "core") for part in (own, after, before)]
    att_high, total_high = f2(meta, qkv, 3)
    far_low, far_high, att_high, *near = tie(far_low, far_high, att_high, *near)
    mine = (own, after, far_low, far_high, before)
    other = (near[0], near[1], swap(far_low, "core"), swap(far_high, "core"), near[2])
    up_order = vecs[8:12].reshape(4, 32, 4, 6).transpose(2, 1, 0, 3).reshape(4, 1, D)

    att_high, up_order = tie(att_high, up_order)
    (
        kept_result,
        sent_result,
        grad_middle,
        grad_attended,
        wide_kept,
        wide_away,
        sums,
        up_sums,
    ) = ff(
        meta,
        image,
        (att_low, att_high),
        cotangent,
        got_cotangent,
        mine,
        other,
        vecs,
        up_order,
    )

    got_wide = swap(wide_away, "core")
    low = b2(meta, qkv, grad_attended, att_low, total_low, 0)
    got_wide, *low = tie(got_wide, *low)
    two = (wide_kept.astype(F32) + got_wide.astype(F32)).astype(BF)
    two, grad_attended = tie(two, grad_attended)
    two = along(two, ZY)

    high = b2(meta, qkv, grad_attended, att_high, total_high, 3)
    sent_result, up_sums, sums, *high = tie(sent_result, up_sums, sums, *high)
    got_result = swap(sent_result, "xl")
    up_sums = up_sums.reshape(4, 32, 4, 6).transpose(2, 1, 0, 3).reshape(4, D)
    small_sums = jnp.concatenate(
        [jnp.zeros((4, D), F32), sums[:4], up_sums, jnp.zeros((4, D), F32)]
    )
    kept_grad, sent_grad, one_kept, one_away = b1(
        meta, image, normed, grad_middle, low, high, one_mine, one_other, vecs, small_sums
    )
    one_kept, one_away, got_result = tie(one_kept, one_away, got_result)
    one = (one_kept.astype(F32) + swap(one_away, "core").astype(F32)).astype(BF)
    one, two = tie(one, two)
    one = along(one, ZY)

    def shrink(parts):
        return jnp.sum(parts.astype(F32), axis=0).astype(BF)

    def plane_of(parts):
        return shrink(parts).reshape(2, 2, 4, 24, parts.shape[-1]).transpose(2, 0, 1, 3, 4)

    two = plane_of(two)
    place = at_other

    def piece(step):
        part = lax.dynamic_index_in_dim(two, (place + step) % 4, 0, keepdims=False)
        if step:
            part = step_along(part, YZ, step)
        return part.astype(F32)

    two = (piece(0) + piece(1) + piece(2) + piece(3)).astype(BF)
    one = shrink(along(plane_of(one), YZ))
    line = jnp.concatenate([one, two], axis=3)
    blocks = jnp.concatenate([line[..., :1408], line[..., 2176:]], axis=3)
    blocks = blocks.reshape(2, 2, 2, 2, 6, 1664).transpose(2, 1, 3, 0, 4, 5).reshape(8, 12, 1664)
    downs = line[..., 1408:2176].transpose(1, 0, 2, 3).reshape(1, 4, 12, 2 * D)
    downs = jnp.concatenate([downs, downs]).reshape(8, 12, 2 * D)
    got = among(jnp.concatenate([blocks, downs], axis=2)).reshape(2, 4, 12, 3200)
    got = jnp.sum(got.astype(F32), axis=1)
    high = cross(got[1].astype(BF)).astype(F32)
    own_down = jnp.where(core == 0, got[0, :, 1664:], high[:, 1664:]).reshape(24, D)
    back = jnp.stack([got[0, :, :1664], high[:, :1664]]).reshape(4, 6, 1664)
    own_one = jnp.moveaxis(back[..., :640], 0, 1).reshape(6, 2560)
    own_up = back[..., 640:1408].reshape(4, 6, 32, 24).transpose(1, 2, 0, 3).reshape(6, FF)
    own_out = jnp.moveaxis(back[..., 1408:1600], 0, 1).reshape(6, D)
    small = own_one[:, 3 * D : 3 * D + 12].T
    return (
        give_back(kept_result, got_result),
        give_back(kept_grad, swap(sent_grad, "xl")),
        own_one[:, : 3 * D],
        own_out,
        own_up,
        own_down,
        small[0],
        small[1],
        small[2],
        small[3],
        small[4],
        small[5],
        small[6],
        small[8:].reshape(24),
        small[7],
    )


def solution(mesh):
    fine = Mesh(mesh.devices.reshape(4, 2, 4, 2, 2), AXES)
    images = ("z", "xh", "y", "core")
    rows, vec = P(AXES, None), P(AXES)
    tokens = P(None, images, "xl", None)
    return jax.shard_map(
        per_device,
        mesh=fine,
        in_specs=(tokens, tokens, P(None, images)) + (rows,) * 4 + (vec,) * 9,
        out_specs=(tokens, tokens) + (rows,) * 4 + (vec,) * 9,
        check_vma=False,
    )
```

```python
import functools
import math

import jax
import jax.numpy as jnp
from jax import lax
from jax.experimental import pallas as pl
from jax.experimental.pallas import tpu as pltpu
from jax.sharding import Mesh
from jax.sharding import PartitionSpec as P

D = 768
FF = 3072
TOK = 290
HALF = 320
ROWS = 2 * HALF
AXES = ("z", "xh", "y", "core", "xl")
BF = jnp.bfloat16
F32 = jnp.float32
F2C = 640
B2C = 640
SUB = 768
FFC = 640
VFF = 60


def mm(a, b):
    return lax.dot_general(a, b, (((1,), (0,)), ((), ())), preferred_element_type=F32)


def mm_nt(a, b):
    return lax.dot_general(a, b, (((1,), (1,)), ((), ())), preferred_element_type=F32)


def mm_tn(a, b):
    return lax.dot_general(a, b, (((0,), (0,)), ((), ())), preferred_element_type=F32)


def unit(values):
    centred = values - jnp.mean(values, axis=-1, keepdims=True)
    inverse = lax.rsqrt(jnp.mean(centred * centred, axis=-1, keepdims=True) + 1e-06)
    return centred * inverse, inverse


def norm_back(e, u, inverse, gain):
    s = e * gain
    mean = jnp.mean(s, axis=-1, keepdims=True)
    return inverse * (s - mean - u * jnp.mean(s * u, axis=-1, keepdims=True))


def call(kernel, meta, grid, ins, outs, scratch=(), us=10, vmem=60):
    return pl.pallas_call(
        kernel,
        grid_spec=pltpu.PrefetchScalarGridSpec(
            num_scalar_prefetch=1,
            grid=grid,
            in_specs=[spec for spec, _ in ins],
            out_specs=[spec for spec, _ in outs],
            scratch_shapes=list(scratch),
        ),
        out_shape=[shape for _, shape in outs],
        cost_estimate=pl.CostEstimate(
            flops=us * 10**9, bytes_accessed=us * 3 * 10**6, transcendentals=0
        ),
        compiler_params=pltpu.CompilerParams(vmem_limit_bytes=vmem * 2**20),
    )(meta, *[array for _, array in ins])


def whole(shape):
    return pl.BlockSpec(shape, lambda *_: (0,) * len(shape))


def sds(shape, dt):
    return jax.ShapeDtypeStruct(shape, dt)


def mine_spec(n):
    return pl.BlockSpec((4, 1, 192, n), lambda j, m: (0, jnp.clip(j - 2 * m[0], 0, 1), 0, 0))


def other_spec(n):
    return pl.BlockSpec((4, 1, 192, n), lambda j, m: (0, jnp.clip(j - 2 + 2 * m[0], 0, 1), 0, 0))


def rows_of(ref, i=0):
    return ref[:, i].reshape(D, ref.shape[-1])


OWN_HALF = pl.BlockSpec((1, 1, TOK, D), lambda j, m: (m[1], 0, 0, 0))
FULL = whole((ROWS, D))


def fill(ref, mine, got):
    ref[0:TOK] = mine
    ref[TOK:HALF] = jnp.zeros((HALF - TOK, D), BF)
    ref[HALF : HALF + TOK] = got
    ref[HALF + TOK :] = jnp.zeros((HALF - TOK, D), BF)


def key_ok(meta, shape, axis):
    slot = lax.broadcasted_iota(jnp.int32, shape, axis)
    half = (slot >= HALF).astype(jnp.int32)
    within = slot - half * HALF
    half = jnp.where(meta[1] == 1, 1 - half, half)
    return jnp.where((within < TOK) & (within + TOK * half < meta[2]), 0.0, -1e30).astype(F32)


def f1_kernel(meta, x_ref, got_ref, sm_ref, so_ref, wm_ref, wo_ref, qkv_ref, n1_ref, vec_ref, im_ref, bias_ref):
    j = pl.program_id(0)

    @pl.when(j == 0)
    def _():
        small = jnp.where(meta[0] == 1, rows_of(sm_ref).astype(F32), rows_of(so_ref).astype(F32))
        vec = small.T[:16]
        vec_ref[...] = vec
        fill(im_ref, x_ref[0, 0], got_ref[...])
        u, _ = unit(im_ref[...].astype(F32))
        n1_ref[...] = (u * vec[0:1] + vec[1:2]).astype(BF)
        bias_ref[...] = jnp.zeros_like(bias_ref)
        bias_ref[0:1, 0:D] = vec[2:3]
        bias_ref[0:1, 2 * D : 3 * D] = vec[3:4]

    b = bias_ref[0:1, pl.ds(pl.multiple_of(j * 640, 128), 640)]
    own = (j // 2) == meta[0]

    @pl.when(own)
    def _():
        qkv_ref[...] = (mm(n1_ref[...], rows_of(wm_ref)) + b).astype(BF)

    @pl.when(jnp.logical_not(own))
    def _():
        qkv_ref[...] = (mm(n1_ref[...], rows_of(wo_ref)) + b).astype(BF)


def f1(meta, x, got, mine, other):
    tail = pl.BlockSpec((4, 1, 192, 128), lambda j, m: (0, 1, 0, 3))
    return call(
        f1_kernel,
        meta,
        (4,),
        [(OWN_HALF, x), (whole((TOK, D)), got), (tail, mine), (tail, other)]
        + [(mine_spec(640), mine), (other_spec(640), other)],
        [
            (pl.BlockSpec((ROWS, 640), lambda j, m: (0, j)), sds((ROWS, 2560), BF)),
            (FULL, sds((ROWS, D), BF)),
            (whole((16, D)), sds((16, D), F32)),
            (FULL, sds((ROWS, D), BF)),
        ],
        [pltpu.VMEM((8, 2560), F32)],
        us=6,
        vmem=24,
    )


def head_block(first):
    return pl.BlockSpec((ROWS, 128), lambda h, m: (0, h + first))


def f2_kernel(meta, q_ref, k_ref, v_ref, o_ref, lse_ref):
    lane0 = lax.broadcasted_iota(jnp.int32, (1, 128), 1) < 64
    k = k_ref[...]
    v = v_ref[...]
    mask = key_ok(meta, (1, ROWS), 1)
    for c in range(0, ROWS, F2C):
        q = q_ref[c : c + F2C] * jnp.asarray(0.125, BF)
        res = []
        for pick in (lane0, ~lane0):
            s = mm_nt(jnp.where(pick, q, jnp.zeros_like(q)), k) + mask
            top = jnp.max(s, axis=-1, keepdims=True)
            p = jnp.exp(s - top)
            total = jnp.sum(p, axis=-1, keepdims=True)
            o = mm(p.astype(BF), v) * (1.0 / total)
            res.append((o, jnp.broadcast_to(top + jnp.log(total), (F2C, 128))))
        o_ref[c : c + F2C] = jnp.where(lane0, res[0][0], res[1][0]).astype(BF)
        lse_ref[c : c + F2C] = jnp.where(lane0, res[0][1], res[1][1])


def f2(meta, qkv, first):
    return call(
        f2_kernel,
        meta,
        (3,),
        [(head_block(first + i), qkv) for i in (0, 6, 12)],
        [(head_block(0), sds((ROWS, D // 2), BF)), (head_block(0), sds((ROWS, D // 2), F32))],
        us=6,
        vmem=24,
    )


def b2_kernel(meta, q_ref, k_ref, v_ref, do_ref, o_ref, lse_ref, dq_ref, dk_ref, dv_ref):
    lane0 = lax.broadcasted_iota(jnp.int32, (1, 128), 1) < 64
    q = q_ref[...] * jnp.asarray(0.125, BF)
    do = do_ref[...]
    lse = lse_ref[...].T
    dd = (do.astype(F32) * o_ref[...].astype(F32)).T
    mask_all = key_ok(meta, (ROWS, 1), 0)
    rows = [
        (lse[0:1], jnp.sum(dd[:64], axis=0, keepdims=True), lane0),
        (lse[64:65], jnp.sum(dd[64:], axis=0, keepdims=True), ~lane0),
    ]
    dq = [None, None]
    for c in range(0, ROWS, B2C):
        k = k_ref[c : c + B2C]
        v = v_ref[c : c + B2C]
        mask = mask_all[c : c + B2C]
        res = []
        for h, (top, inner, pick) in enumerate(rows):
            kh = jnp.where(pick, k, jnp.zeros_like(k))
            vh = jnp.where(pick, v, jnp.zeros_like(v))
            p = jnp.exp(mm_nt(kh, q) + mask - top)
            ds = (p * (mm_nt(vh, do) - inner)).astype(BF)
            res.append((mm(ds, q), mm(p.astype(BF), do)))
            t = mm_tn(ds, k)
            dq[h] = t if c == 0 else dq[h] + t
        dk_ref[c : c + B2C] = jnp.where(lane0, res[0][0], res[1][0]).astype(BF)
        dv_ref[c : c + B2C] = jnp.where(lane0, res[0][1], res[1][1]).astype(BF)
    dq_ref[...] = (jnp.where(lane0, dq[0], dq[1]) * 0.125).astype(BF)


def b2(meta, qkv, do, o, lse, first):
    return call(
        b2_kernel,
        meta,
        (3,),
        [(head_block(first + i), qkv) for i in (0, 6, 12)]
        + [(head_block(first), do), (head_block(0), o), (head_block(0), lse)],
        [(head_block(0), sds((ROWS, D // 2), BF))] * 3,
        us=9,
    )


ERF_TOP = (0.00022905065861350646, 0.0034082910107109506, 0.050955695062380861)
ERF_TOP += (0.18520832239976145, 1.128379143519084)
ERF_LOW = (-1.1791602954361697e-7, 0.000023547966471313185, 0.0010179625278914885)
ERF_LOW += (0.014070470171167667, 0.11098505178285362, 0.49746925110067538, 1.0)


def erf(x):
    x = jnp.clip(x, -3.832506856900711, 3.832506856900711)
    y = x * x
    top = y * ERF_TOP[0] + ERF_TOP[1]
    for a in ERF_TOP[2:]:
        top = top * y + a
    low = y * ERF_LOW[0] + ERF_LOW[1]
    for b in ERF_LOW[2:]:
        low = low * y + b
    r = pl.reciprocal(low, approx=True)
    r = r * (2.0 - low * r)
    return x * top * r


def ff_kernel(
    meta, x_ref, att_a, att_b, gm_in, gg_in, vec_ref, ub_ref, wm0, wm1, wm2, wm3, wm4, wo0, wo1, wo2, wo3, wo4,
    keep_ref, send_ref, gm_ref, ga_ref, grad_m, grad_o, sums_ref, dub_ref,
    mid, inv, n2, act, gh, acc, e2, g_low, w_out, w_buf, g_buf, o_buf, w_sem, g_sem, o_sem,
):
    j = pl.program_id(0)
    core = meta[0]

    def each(count, body):
        lax.fori_loop(0, count, lambda k, _: (body(k), 0)[1], 0)

    def rows(k):
        return pl.ds(pl.multiple_of(k * FFC, FFC), FFC)

    pieces = (((wm0, wm1, wm2, wm3, wm4), core, meta[3]), ((wo0, wo1, wo2, wo3, wo4), 1 - core, meta[4]))

    def fetch(block, act_on):
        slot = block % 2

        def copy_all(parts, at, half):
            own, after, far_low, far_high, before = parts
            for k, src in enumerate((own.at[half], after.at[half], (far_low, far_high)[half], before.at[half])):
                act_on(
                    pltpu.make_async_copy(
                        src.at[:, : 2 * D], w_buf.at[half, (at + k) % 4], w_sem.at[half, k]
                    )
                )

        for parts, owner, at in pieces:
            for half in range(2):
                here = ((block // 2) == owner) & (slot == half)
                pl.when(here)(functools.partial(copy_all, parts, at, half))

    def flush(block, act_on):
        slot = block % 2
        for refs, mine in ((grad_m, True), (grad_o, False)):
            copy = pltpu.make_async_copy(
                g_buf.at[slot], refs.at[:, slot, :, : 2 * D], g_sem.at[slot]
            )
            pl.when(((block // 2) == core) == mine)(lambda: act_on(copy))

    start = lambda copy: copy.start()
    wait = lambda copy: copy.wait()
    out_in = []
    for k, (parts, owner, at) in enumerate(pieces):
        own, after, far_low, far_high, before = parts
        moves = [(own, 0, None), (after, 1, None), (far_low, 2, 0), (far_high, 2, 1), (before, 3, None)]
        for q, (src, step, half) in enumerate(moves):
            dst = o_buf.at[owner, (at + step) % 4]
            src = src.at[:, 2 * D :] if half is not None else src.at[:, :, 2 * D :]
            dst = dst if half is None else dst.at[half]
            out_in.append(pltpu.make_async_copy(src, dst, o_sem.at[5 * k + q]))
    out_back = [
        pltpu.make_async_copy(o_buf.at[place], refs.at[:, :, :, 2 * D :], o_sem.at[k])
        for k, (refs, place) in enumerate(((grad_m, core), (grad_o, 1 - core)))
    ]

    @pl.when(j == 0)
    def _():
        for copy in out_in:
            copy.start()
        fetch(j, start)
        fill(g_low, gm_in[meta[1], 0], gg_in[...])
        acc[...] = jnp.zeros_like(acc)
        e2[...] = jnp.zeros_like(e2)
        for copy in out_in:
            copy.wait()
        for i in range(4):
            w_out[:, 192 * i : 192 * i + 192] = o_buf[i // 2, :, i % 2, :, :192].reshape(D, 192)

        def body(k):
            r = rows(k)
            branch = mm(att_a[r], w_out[: D // 2]) + mm(att_b[r], w_out[D // 2 :])
            m = x_ref[r].astype(F32) + (branch + vec_ref[4:5])
            mid[r] = m
            u, i = unit(m)
            inv[r] = jnp.broadcast_to(i, (FFC, 128))
            n2[r] = (u * vec_ref[5:6] + vec_ref[6:7]).astype(BF)

        each(ROWS // FFC, body)

    @pl.when(j < 4)
    def _():
        slot = j % 2
        fetch(j, wait)
        pl.when(j < 3)(lambda: fetch(j + 1, start))
        pl.when(j >= 2)(lambda: flush(j - 2, wait))
        dub_ref[j] = jnp.zeros((1, D), F32)

        def body(k):
            r = rows(k)
            for c in range(0, D, SUB):
                cols = slice(c, c + SUB)
                up = w_buf[slot, :, :, cols].reshape(D, SUB)
                down = w_buf[slot, c // 192 : (c + SUB) // 192, :, D:].reshape(SUB, D)
                h = mm(n2[r], up) + ub_ref[j, :, cols]
                t = mm_nt(g_low[r], down)
                phi = 0.5 + 0.5 * erf(h * math.sqrt(0.5))
                act[r, cols] = (h * phi).astype(BF)
                slope = phi + h * (jnp.exp(h * h * -0.5) * (1.0 / math.sqrt(2.0 * math.pi)))
                t = (t * slope).astype(BF)
                gh[r, cols] = t
                dub_ref[j, :, cols] += jnp.sum(t.astype(F32), axis=0, keepdims=True)
            acc[r] += mm(act[r], w_buf[slot, :, :, D:].reshape(D, D))
            e2[r] += mm_nt(gh[r], w_buf[slot, :, :, :D].reshape(D, D))

        each(ROWS // FFC, body)

        def grads(k):
            c = pl.multiple_of(k * SUB, SUB)
            t = mm_tn(act[:, pl.ds(c, SUB)], g_low[...]).astype(BF)
            g_buf[slot, pl.ds(k * (SUB // 192), SUB // 192), :, D:] = t.reshape(-1, 192, D)
            t = mm_tn(n2[...], gh[:, pl.ds(c, SUB)]).astype(BF)
            g_buf[slot, :, :, pl.ds(c, SUB)] = t.reshape(4, 192, SUB)

        each(D // SUB, grads)
        flush(j, start)

    @pl.when(j == 4)
    def _():
        flush(j - 2, wait)
        sums_ref[...] = jnp.zeros_like(sums_ref)

        def body(k):
            r = rows(k)
            m = mid[r]
            res = (m + (acc[r] + vec_ref[7:8])).astype(BF)
            keep_ref[...] = res[:TOK]
            send_ref[...] = res[HALF : HALF + TOK]
            g = g_low[r].astype(F32)
            e = e2[r]
            i = inv[r][:, 0:1]
            u = (m - jnp.mean(m, axis=-1, keepdims=True)) * i
            grad = g + norm_back(e, u, i, vec_ref[5:6])
            gm_ref[r] = grad
            low = grad.astype(BF)
            n2[r] = low
            ga_ref[r] = mm_nt(low, w_out[...]).astype(BF)
            for q, t in enumerate((low.astype(F32), e * u, e, g)):
                sums_ref[q : q + 1] += jnp.sum(t, axis=0, keepdims=True)

        each(ROWS // FFC, body)
        grad_out = jnp.concatenate([mm_tn(att[...], n2[...]) for att in (att_a, att_b)])
        grad_out = grad_out.astype(BF)
        for i in range(4):
            part = grad_out[:, 192 * i : 192 * i + 192].reshape(4, 192, 192)
            o_buf[i // 2, :, i % 2, :, :192] = part
            o_buf[i // 2, :, i % 2, :, 192:] = jnp.zeros((4, 192, 64), BF)
        for copy in out_back:
            copy.start()
        flush(j - 1, wait)
        for copy in out_back:
            copy.wait()


def add_kernel(meta, left_ref, right_ref, sum_ref):
    sum_ref[...] = (left_ref[...].astype(F32) + right_ref[...].astype(F32)).astype(BF)


def add(meta, left, right):
    n = left.shape[3]
    part = pl.BlockSpec((1, 1, 192, n), lambda i, m: (i // 2, i % 2, 0, 0))
    out = [(part, sds(left.shape, BF))]
    return call(add_kernel, meta, (8,), [(part, left), (part, right)], out, us=5)[0]


def ff(meta, x, att, cot, cot_got, mine, other, vec, up_bias):
    any_ref = pl.BlockSpec(memory_space=pl.ANY)
    wide = (any_ref, sds((4, 2, 192, 1792), BF))
    half = (whole((TOK, D)), sds((TOK, D), BF))
    ins = [(FULL, x)] + [(whole((ROWS, D // 2)), part) for part in att]
    ins += [(whole((2, 1, TOK, D)), cot), (whole((TOK, D)), cot_got)]
    ins += [(whole((16, D)), vec), (whole((4, 1, D)), up_bias)]
    ins += [(any_ref, piece) for piece in (*mine, *other)]
    outs = [half, half, (FULL, sds((ROWS, D), F32)), (FULL, sds((ROWS, D), BF)), wide, wide]
    outs += [(whole((8, D)), sds((8, D), F32)), (whole((4, 1, D)), sds((4, 1, D), F32))]
    return call(
        ff_kernel,
        meta,
        (5,),
        ins,
        outs,
        [pltpu.VMEM((ROWS, D), F32), pltpu.VMEM((ROWS, 128), F32), pltpu.VMEM((ROWS, D), BF)]
        + [pltpu.VMEM((ROWS, D), BF)] * 2
        + [pltpu.VMEM((ROWS, D), F32)] * 2
        + [pltpu.VMEM((ROWS, D), BF), pltpu.VMEM((D, D), BF)]
        + [pltpu.VMEM((2, 4, 192, 2 * D), BF)] * 2
        + [pltpu.VMEM((2, 4, 2, 192, 256), BF)]
        + [pltpu.SemaphoreType.DMA((2, 4)), pltpu.SemaphoreType.DMA((2,)), pltpu.SemaphoreType.DMA((10,))],
        us=36,
        vmem=VFF,
    )


def b1_kernel(
    meta, x_ref, n1_ref, gm_ref, qa_ref, ka_ref, va_ref, qb_ref, kb_ref, vb_ref, wm_ref, wo_ref, vec_ref, small_ref,
    keep_ref, send_ref, gwm_ref, gwo_ref, gj, e1,
):
    j = pl.program_id(0)
    core = meta[0]

    @pl.when(j == 0)
    def _():
        gj[0, :, 0:384] = qa_ref[...]
        gj[0, :, 384:640] = qb_ref[:, 0:256]
        gj[1, :, 0:128] = qb_ref[:, 256:384]
        gj[1, :, 128:512] = ka_ref[...]
        gj[1, :, 512:640] = kb_ref[:, 0:128]
        gj[2, :, 0:256] = kb_ref[:, 128:384]
        gj[2, :, 256:640] = va_ref[...]
        gj[3, :, 0:384] = vb_ref[...]
        gj[3, :, 384:640] = jnp.zeros((ROWS, 256), BF)
        e1[...] = jnp.zeros_like(e1)

    b = gj[j]

    def block(w_ref, grad_ref):
        e1[...] += mm_nt(b, rows_of(w_ref))
        grad_ref[:, 0] = mm_tn(n1_ref[...], b).astype(BF).reshape(4, 192, 640)

    own = (j // 2) == core
    pl.when(own)(lambda: block(wm_ref, gwm_ref))
    pl.when(jnp.logical_not(own))(lambda: block(wo_ref, gwo_ref))

    @pl.when(j == 3)
    def _():
        tot = [None] * 4
        for c in range(2):
            r = slice(c * HALF, (c + 1) * HALF)
            u, i = unit(x_ref[r].astype(F32))
            e = e1[r]
            grad = gm_ref[r] + norm_back(e, u, i, vec_ref[0:1])
            if c == 0:
                keep_ref[...] = grad[:TOK]
            else:
                send_ref[...] = grad[:TOK].astype(BF)
            sides = [
                jnp.concatenate([left[r], right[r]], axis=1).astype(F32)
                for left, right in ((qa_ref, qb_ref), (va_ref, vb_ref))
            ]
            for k, t in enumerate((e * u, e, *sides)):
                t = jnp.sum(t, axis=0, keepdims=True)
                tot[k] = t if c == 0 else tot[k] + t
        rows = jnp.concatenate(tot + [small_ref[4:16], jnp.zeros((112, D), F32)], axis=0)
        cols = rows.T.astype(BF)

        def put(ref):
            ref[:, 0, :, 384:512] = cols.reshape(4, 192, 128)

        pl.when(core == 1)(lambda: put(gwm_ref))
        pl.when(core == 0)(lambda: put(gwo_ref))


def b1(meta, x, n1, gm, low, high, mine, other, vec, small):
    pair = [(spec(640), sds((4, 2, 192, 640), BF)) for spec in (mine_spec, other_spec)]
    return call(
        b1_kernel,
        meta,
        (4,),
        [(FULL, x), (FULL, n1), (FULL, gm)]
        + [(whole((ROWS, D // 2)), part) for part in (*low, *high)]
        + [(mine_spec(640), mine), (other_spec(640), other), (whole((16, D)), vec), (whole((16, D)), small)],
        [(whole((TOK, D)), sds((TOK, D), F32)), (whole((TOK, D)), sds((TOK, D), BF))] + pair,
        [pltpu.VMEM((4, ROWS, 640), BF), pltpu.VMEM((ROWS, D), F32)],
        us=12,
    )


def ring_groups(axis_zero, axis_one):
    groups = []
    for core, axis in ((0, axis_zero), (1, axis_one)):
        others = [name for name in "zxy" if name != axis]
        for i in range(4):
            for j in range(4):
                at = {others[0]: i, others[1]: j}
                line = []
                for k in range(4):
                    at[axis] = k
                    z, x, y = at["z"], at["x"], at["y"]
                    line.append((((z * 2 + x // 2) * 4 + y) * 2 + core) * 2 + x % 2)
                groups.append(line)
    return groups


ZY = ring_groups("z", "y")
YZ = ring_groups("y", "z")


def swap(value, axis):
    return lax.ppermute(value, axis, [(0, 1), (1, 0)])


def tie(*values):
    return lax.optimization_barrier(values)


CROSS = [(4 * i + k, 4 * k + i) for i in range(4) for k in range(4)]


def cross(value):
    return lax.ppermute(value, ("z", "y"), CROSS)


def along(value, groups):
    return lax.all_to_all(value, AXES, 0, 0, tiled=True, axis_index_groups=groups)


def copies(value, groups):
    return along(jnp.broadcast_to(value[None], (4, *value.shape)), groups)


def step_along(value, groups, step):
    pairs = [(line[i], line[(i + step) % 4]) for line in groups for i in range(4)]
    return lax.ppermute(value, AXES, pairs)


def among(value):
    return lax.all_to_all(value, ("core", "xh", "xl"), 0, 0, tiled=True)


def per_device(
    inputs,
    cotangent,
    lengths,
    w_qkv,
    w_out,
    w_up,
    w_down,
    ln1_gain,
    ln1_shift,
    q_bias,
    v_bias,
    out_bias,
    ln2_gain,
    ln2_shift,
    up_bias,
    down_bias,
):
    side = lax.axis_index("xl")
    core = lax.axis_index("core")

    def theirs(block):
        return swap(lax.dynamic_index_in_dim(block, 1 - side, 0, keepdims=False)[0], "xl")

    def give_back(kept, got):
        got = got.astype(kept.dtype)
        first = side == 0
        return jnp.stack([jnp.where(first, kept, got), jnp.where(first, got, kept)])[:, None]

    got_image = theirs(inputs)

    row = lax.broadcasted_iota(jnp.int32, (12, 6), 0)
    smalls = jnp.pad(up_bias.reshape(4, 6), ((8, 0), (0, 0)))
    for i, part in enumerate(
        (ln1_gain, ln1_shift, q_bias, v_bias, out_bias, ln2_gain, ln2_shift, down_bias)
    ):
        smalls = jnp.where(row == i, part[None], smalls)
    wide_one = jnp.concatenate([w_qkv, smalls.T, jnp.zeros((6, 244), BF)], axis=1)
    cut_out = jnp.pad(w_out.reshape(6, 4, 192), ((0, 0), (0, 0), (0, 64)))
    cut_up = w_up.reshape(6, 32, 4, 24).transpose(0, 2, 1, 3).reshape(6, 4, D)
    cut = jnp.concatenate([wide_one.reshape(6, 4, 640), cut_up, cut_out], axis=2)
    cut = jnp.moveaxis(cut, 1, 0).reshape(2, 12, 1664)
    cut = jnp.concatenate([cut, jnp.stack([w_down.reshape(12, 2 * D)] * 2)], axis=2)
    sent = jnp.stack([cut[0]] * 4 + [cross(cut[1])] * 4)
    line = among(sent)
    blocks = line[..., :1664].reshape(2, 2, 2, 2, 6, 1664).transpose(3, 1, 0, 2, 4, 5)
    downs = lax.dynamic_index_in_dim(line.reshape(2, 2, 2, 12, 3200), core, 0, keepdims=False)
    downs = downs[..., 1664:].reshape(2, 2, 24, D).transpose(1, 0, 2, 3)
    blocks = blocks.reshape(2, 2, 24, 1664)
    line = jnp.concatenate([blocks[..., :1408], downs, blocks[..., 1408:]], axis=3)
    plane = copies(line, YZ).transpose(1, 2, 0, 3, 4).reshape(384, 2432)
    plane, got_image = tie(plane, got_image)
    one_mine = copies(plane[:, :640], ZY).reshape(4, 2, 192, 640)
    own = plane[:, 640:].reshape(2, 192, 1792)
    got_cotangent = theirs(cotangent)
    length = lax.dynamic_index_in_dim(lengths, side, 0, keepdims=False)[0]
    z, y = lax.axis_index("z"), lax.axis_index("y")
    at_mine, at_other = jnp.where(core == 0, z, y), jnp.where(core == 0, y, z)
    meta = jnp.stack([core, side, length, at_mine, at_other]).astype(jnp.int32)
    own, one_mine, got_cotangent, meta = tie(own, one_mine, got_cotangent, meta)
    one_other = swap(one_mine, "core")
    before, after = step_along(own, ZY, 1), step_along(own, ZY, 3)

    qkv, normed, vecs, image = f1(meta, inputs, got_image, one_mine, one_other)
    att_low, total_low = f2(meta, qkv, 0)
    before, after, qkv, att_low = tie(before, after, qkv, att_low)
    far_low, far_high = step_along(before[0], ZY, 1), step_along(after[1], ZY, 3)
    near = [swap(part, "core") for part in (own, after, before)]
    att_high, total_high = f2(meta, qkv, 3)
    far_low, far_high, att_high, *near = tie(far_low, far_high, att_high, *near)
    mine = (own, after, far_low, far_high, before)
    other = (near[0], near[1], swap(far_low, "core"), swap(far_high, "core"), near[2])
    up_order = vecs[8:12].reshape(4, 32, 4, 6).transpose(2, 1, 0, 3).reshape(4, 1, D)

    att_high, up_order = tie(att_high, up_order)
    (
        kept_result,
        sent_result,
        grad_middle,
        grad_attended,
        wide_kept,
        wide_away,
        sums,
        up_sums,
    ) = ff(
        meta,
        image,
        (att_low, att_high),
        cotangent,
        got_cotangent,
        mine,
        other,
        vecs,
        up_order,
    )

    got_wide = swap(wide_away, "core")
    low = b2(meta, qkv, grad_attended, att_low, total_low, 0)
    got_wide, *low = tie(got_wide, *low)
    two = add(meta, wide_kept, got_wide)
    two, grad_attended = tie(two, grad_attended)
    two = along(two, ZY)

    high = b2(meta, qkv, grad_attended, att_high, total_high, 3)
    sent_result, up_sums, sums, *high = tie(sent_result, up_sums, sums, *high)
    got_result = swap(sent_result, "xl")
    up_sums = up_sums.reshape(4, 32, 4, 6).transpose(2, 1, 0, 3).reshape(4, D)
    small_sums = jnp.concatenate(
        [jnp.zeros((4, D), F32), sums[:4], up_sums, jnp.zeros((4, D), F32)]
    )
    kept_grad, sent_grad, one_kept, one_away = b1(
        meta, image, normed, grad_middle, low, high, one_mine, one_other, vecs, small_sums
    )
    one_kept, one_away, got_result = tie(one_kept, one_away, got_result)
    one = (one_kept.astype(F32) + swap(one_away, "core").astype(F32)).astype(BF)
    one, two = tie(one, two)
    one = along(one, ZY)

    def shrink(parts):
        return jnp.sum(parts.astype(F32), axis=0).astype(BF)

    def plane_of(parts):
        return shrink(parts).reshape(2, 2, 4, 24, parts.shape[-1]).transpose(2, 0, 1, 3, 4)

    two = plane_of(two)
    place = at_other

    def piece(step):
        part = lax.dynamic_index_in_dim(two, (place + step) % 4, 0, keepdims=False)
        if step:
            part = step_along(part, YZ, step)
        return part.astype(F32)

    two = (piece(0) + piece(1) + piece(2) + piece(3)).astype(BF)
    one = shrink(along(plane_of(one), YZ))
    line = jnp.concatenate([one, two], axis=3)
    blocks = jnp.concatenate([line[..., :1408], line[..., 2176:]], axis=3)
    blocks = blocks.reshape(2, 2, 2, 2, 6, 1664).transpose(2, 1, 3, 0, 4, 5).reshape(8, 12, 1664)
    downs = line[..., 1408:2176].transpose(1, 0, 2, 3).reshape(1, 4, 12, 2 * D)
    downs = jnp.concatenate([downs, downs]).reshape(8, 12, 2 * D)
    got = among(jnp.concatenate([blocks, downs], axis=2)).reshape(2, 4, 12, 3200)
    got = jnp.sum(got.astype(F32), axis=1)
    high = cross(got[1].astype(BF)).astype(F32)
    own_down = jnp.where(core == 0, got[0, :, 1664:], high[:, 1664:]).reshape(24, D)
    back = jnp.stack([got[0, :, :1664], high[:, :1664]]).reshape(4, 6, 1664)
    own_one = jnp.moveaxis(back[..., :640], 0, 1).reshape(6, 2560)
    own_up = back[..., 640:1408].reshape(4, 6, 32, 24).transpose(1, 2, 0, 3).reshape(6, FF)
    own_out = jnp.moveaxis(back[..., 1408:1600], 0, 1).reshape(6, D)
    small = own_one[:, 3 * D : 3 * D + 12].T
    return (
        give_back(kept_result, got_result),
        give_back(kept_grad, swap(sent_grad, "xl")),
        own_one[:, : 3 * D],
        own_out,
        own_up,
        own_down,
        small[0],
        small[1],
        small[2],
        small[3],
        small[4],
        small[5],
        small[6],
        small[8:].reshape(24),
        small[7],
    )


def solution(mesh):
    fine = Mesh(mesh.devices.reshape(4, 2, 4, 2, 2), AXES)
    images = ("z", "xh", "y", "core")
    rows, vec = P(AXES, None), P(AXES)
    tokens = P(None, images, "xl", None)
    return jax.shard_map(
        per_device,
        mesh=fine,
        in_specs=(tokens, tokens, P(None, images)) + (rows,) * 4 + (vec,) * 9,
        out_specs=(tokens, tokens) + (rows,) * 4 + (vec,) * 9,
        check_vma=False,
    )
```

```python
import functools
import math

import jax
import jax.numpy as jnp
from jax import lax
from jax.experimental import pallas as pl
from jax.experimental.pallas import tpu as pltpu
from jax.sharding import Mesh
from jax.sharding import PartitionSpec as P

D = 768
FF = 3072
TOK = 290
HALF = 320
ROWS = 2 * HALF
AXES = ("z", "xh", "y", "core", "xl")
BF = jnp.bfloat16
F32 = jnp.float32
F2C = 640
B2C = 640
SUB = 768
FFC = 640
VFF = 60


def mm(a, b):
    return lax.dot_general(a, b, (((1,), (0,)), ((), ())), preferred_element_type=F32)


def mm_nt(a, b):
    return lax.dot_general(a, b, (((1,), (1,)), ((), ())), preferred_element_type=F32)


def mm_tn(a, b):
    return lax.dot_general(a, b, (((0,), (0,)), ((), ())), preferred_element_type=F32)


def unit(values):
    centred = values - jnp.mean(values, axis=-1, keepdims=True)
    inverse = lax.rsqrt(jnp.mean(centred * centred, axis=-1, keepdims=True) + 1e-06)
    return centred * inverse, inverse


def norm_back(e, u, inverse, gain):
    s = e * gain
    mean = jnp.mean(s, axis=-1, keepdims=True)
    return inverse * (s - mean - u * jnp.mean(s * u, axis=-1, keepdims=True))


def call(kernel, meta, grid, ins, outs, scratch=(), us=10, vmem=60):
    return pl.pallas_call(
        kernel,
        grid_spec=pltpu.PrefetchScalarGridSpec(
            num_scalar_prefetch=1,
            grid=grid,
            in_specs=[spec for spec, _ in ins],
            out_specs=[spec for spec, _ in outs],
            scratch_shapes=list(scratch),
        ),
        out_shape=[shape for _, shape in outs],
        cost_estimate=pl.CostEstimate(
            flops=us * 10**9, bytes_accessed=us * 3 * 10**6, transcendentals=0
        ),
        compiler_params=pltpu.CompilerParams(vmem_limit_bytes=vmem * 2**20),
    )(meta, *[array for _, array in ins])


def whole(shape):
    return pl.BlockSpec(shape, lambda *_: (0,) * len(shape))


def sds(shape, dt):
    return jax.ShapeDtypeStruct(shape, dt)


def mine_spec(n):
    return pl.BlockSpec((4, 1, 192, n), lambda j, m: (0, jnp.clip(j - 2 * m[0], 0, 1), 0, 0))


def other_spec(n):
    return pl.BlockSpec((4, 1, 192, n), lambda j, m: (0, jnp.clip(j - 2 + 2 * m[0], 0, 1), 0, 0))


def rows_of(ref, i=0):
    return ref[:, i].reshape(D, ref.shape[-1])


OWN_HALF = pl.BlockSpec((1, 1, TOK, D), lambda j, m: (m[1], 0, 0, 0))
FULL = whole((ROWS, D))


def fill(ref, mine, got):
    ref[0:TOK] = mine
    ref[TOK:HALF] = jnp.zeros((HALF - TOK, D), BF)
    ref[HALF : HALF + TOK] = got
    ref[HALF + TOK :] = jnp.zeros((HALF - TOK, D), BF)


def key_ok(meta, shape, axis):
    slot = lax.broadcasted_iota(jnp.int32, shape, axis)
    half = (slot >= HALF).astype(jnp.int32)
    within = slot - half * HALF
    half = jnp.where(meta[1] == 1, 1 - half, half)
    return jnp.where((within < TOK) & (within + TOK * half < meta[2]), 0.0, -1e30).astype(F32)


def f1_kernel(meta, x_ref, got_ref, sm_ref, so_ref, wm_ref, wo_ref, qkv_ref, n1_ref, vec_ref, im_ref, bias_ref):
    j = pl.program_id(0)

    @pl.when(j == 0)
    def _():
        small = jnp.where(meta[0] == 1, rows_of(sm_ref).astype(F32), rows_of(so_ref).astype(F32))
        vec = small.T[:16]
        vec_ref[...] = vec
        fill(im_ref, x_ref[0, 0], got_ref[...])
        u, _ = unit(im_ref[...].astype(F32))
        n1_ref[...] = (u * vec[0:1] + vec[1:2]).astype(BF)
        bias_ref[...] = jnp.zeros_like(bias_ref)
        bias_ref[0:1, 0:D] = vec[2:3]
        bias_ref[0:1, 2 * D : 3 * D] = vec[3:4]

    b = bias_ref[0:1, pl.ds(pl.multiple_of(j * 640, 128), 640)]
    own = (j // 2) == meta[0]

    @pl.when(own)
    def _():
        qkv_ref[...] = (mm(n1_ref[...], rows_of(wm_ref)) + b).astype(BF)

    @pl.when(jnp.logical_not(own))
    def _():
        qkv_ref[...] = (mm(n1_ref[...], rows_of(wo_ref)) + b).astype(BF)


def f1(meta, x, got, mine, other):
    tail = pl.BlockSpec((4, 1, 192, 128), lambda j, m: (0, 1, 0, 3))
    return call(
        f1_kernel,
        meta,
        (4,),
        [(OWN_HALF, x), (whole((TOK, D)), got), (tail, mine), (tail, other)]
        + [(mine_spec(640), mine), (other_spec(640), other)],
        [
            (pl.BlockSpec((ROWS, 640), lambda j, m: (0, j)), sds((ROWS, 2560), BF)),
            (FULL, sds((ROWS, D), BF)),
            (whole((16, D)), sds((16, D), F32)),
            (FULL, sds((ROWS, D), BF)),
        ],
        [pltpu.VMEM((8, 2560), F32)],
        us=6,
        vmem=24,
    )


def head_block(first):
    return pl.BlockSpec((ROWS, 128), lambda h, m: (0, h + first))


def f2_kernel(meta, q_ref, k_ref, v_ref, o_ref, lse_ref):
    lane0 = lax.broadcasted_iota(jnp.int32, (1, 128), 1) < 64
    k = k_ref[...]
    v = v_ref[...]
    mask = key_ok(meta, (1, ROWS), 1)
    for c in range(0, ROWS, F2C):
        q = q_ref[c : c + F2C] * jnp.asarray(0.125, BF)
        res = []
        for pick in (lane0, ~lane0):
            s = mm_nt(jnp.where(pick, q, jnp.zeros_like(q)), k) + mask
            top = jnp.max(s, axis=-1, keepdims=True)
            p = jnp.exp(s - top)
            total = jnp.sum(p, axis=-1, keepdims=True)
            o = mm(p.astype(BF), v) * (1.0 / total)
            res.append((o, jnp.broadcast_to(top + jnp.log(total), (F2C, 128))))
        o_ref[c : c + F2C] = jnp.where(lane0, res[0][0], res[1][0]).astype(BF)
        lse_ref[c : c + F2C] = jnp.where(lane0, res[0][1], res[1][1])


def f2(meta, qkv, first):
    return call(
        f2_kernel,
        meta,
        (3,),
        [(head_block(first + i), qkv) for i in (0, 6, 12)],
        [(head_block(0), sds((ROWS, D // 2), BF)), (head_block(0), sds((ROWS, D // 2), F32))],
        us=6,
        vmem=24,
    )


def b2_kernel(meta, q_ref, k_ref, v_ref, do_ref, o_ref, lse_ref, dq_ref, dk_ref, dv_ref):
    lane0 = lax.broadcasted_iota(jnp.int32, (1, 128), 1) < 64
    q = q_ref[...] * jnp.asarray(0.125, BF)
    do = do_ref[...]
    lse = lse_ref[...].T
    dd = (do.astype(F32) * o_ref[...].astype(F32)).T
    mask_all = key_ok(meta, (ROWS, 1), 0)
    rows = [
        (lse[0:1], jnp.sum(dd[:64], axis=0, keepdims=True), lane0),
        (lse[64:65], jnp.sum(dd[64:], axis=0, keepdims=True), ~lane0),
    ]
    dq = [None, None]
    for c in range(0, ROWS, B2C):
        k = k_ref[c : c + B2C]
        v = v_ref[c : c + B2C]
        mask = mask_all[c : c + B2C]
        res = []
        for h, (top, inner, pick) in enumerate(rows):
            kh = jnp.where(pick, k, jnp.zeros_like(k))
            vh = jnp.where(pick, v, jnp.zeros_like(v))
            p = jnp.exp(mm_nt(kh, q) + mask - top)
            ds = (p * (mm_nt(vh, do) - inner)).astype(BF)
            res.append((mm(ds, q), mm(p.astype(BF), do)))
            t = mm_tn(ds, k)
            dq[h] = t if c == 0 else dq[h] + t
        dk_ref[c : c + B2C] = jnp.where(lane0, res[0][0], res[1][0]).astype(BF)
        dv_ref[c : c + B2C] = jnp.where(lane0, res[0][1], res[1][1]).astype(BF)
    dq_ref[...] = (jnp.where(lane0, dq[0], dq[1]) * 0.125).astype(BF)


def b2(meta, qkv, do, o, lse, first):
    return call(
        b2_kernel,
        meta,
        (3,),
        [(head_block(first + i), qkv) for i in (0, 6, 12)]
        + [(head_block(first), do), (head_block(0), o), (head_block(0), lse)],
        [(head_block(0), sds((ROWS, D // 2), BF))] * 3,
        us=9,
    )


ERF_TOP = (0.00022905065861350646, 0.0034082910107109506, 0.050955695062380861)
ERF_TOP += (0.18520832239976145, 1.128379143519084)
ERF_LOW = (-1.1791602954361697e-7, 0.000023547966471313185, 0.0010179625278914885)
ERF_LOW += (0.014070470171167667, 0.11098505178285362, 0.49746925110067538, 1.0)


def erf(x):
    x = jnp.clip(x, -3.832506856900711, 3.832506856900711)
    y = x * x
    top = y * ERF_TOP[0] + ERF_TOP[1]
    for a in ERF_TOP[2:]:
        top = top * y + a
    low = y * ERF_LOW[0] + ERF_LOW[1]
    for b in ERF_LOW[2:]:
        low = low * y + b
    r = pl.reciprocal(low, approx=True)
    r = r * (2.0 - low * r)
    return x * top * r


def ff_kernel(
    meta, x_ref, att_a, att_b, gm_in, gg_in, vec_ref, ub_ref, wm0, wm1, wm2, wm3, wm4, wo0, wo1, wo2, wo3, wo4,
    keep_ref, send_ref, gm_ref, ga_ref, grad_m, grad_o, sums_ref, dub_ref,
    mid, inv, n2, act, gh, acc, e2, g_low, w_out, w_buf, g_buf, o_buf, w_sem, g_sem, o_sem,
):
    j = pl.program_id(0)
    core = meta[0]

    def each(count, body):
        lax.fori_loop(0, count, lambda k, _: (body(k), 0)[1], 0)

    def rows(k):
        return pl.ds(pl.multiple_of(k * FFC, FFC), FFC)

    pieces = (((wm0, wm1, wm2, wm3, wm4), core, meta[3]), ((wo0, wo1, wo2, wo3, wo4), 1 - core, meta[4]))

    def fetch(block, act_on):
        slot = block % 2

        def copy_all(parts, at, half):
            own, after, far_low, far_high, before = parts
            for k, src in enumerate((own.at[half], after.at[half], (far_low, far_high)[half], before.at[half])):
                act_on(
                    pltpu.make_async_copy(
                        src.at[:, : 2 * D], w_buf.at[half, (at + k) % 4], w_sem.at[half, k]
                    )
                )

        for parts, owner, at in pieces:
            for half in range(2):
                here = ((block // 2) == owner) & (slot == half)
                pl.when(here)(functools.partial(copy_all, parts, at, half))

    def flush(block, act_on):
        slot = block % 2
        for refs, mine in ((grad_m, True), (grad_o, False)):
            copy = pltpu.make_async_copy(
                g_buf.at[slot], refs.at[:, slot, :, : 2 * D], g_sem.at[slot]
            )
            pl.when(((block // 2) == core) == mine)(lambda: act_on(copy))

    start = lambda copy: copy.start()
    wait = lambda copy: copy.wait()
    out_in = []
    for k, (parts, owner, at) in enumerate(pieces):
        own, after, far_low, far_high, before = parts
        moves = [(own, 0, None), (after, 1, None), (far_low, 2, 0), (far_high, 2, 1), (before, 3, None)]
        for q, (src, step, half) in enumerate(moves):
            dst = o_buf.at[owner, (at + step) % 4]
            src = src.at[:, 2 * D :] if half is not None else src.at[:, :, 2 * D :]
            dst = dst if half is None else dst.at[half]
            out_in.append(pltpu.make_async_copy(src, dst, o_sem.at[5 * k + q]))
    out_back = [
        pltpu.make_async_copy(o_buf.at[place], refs.at[:, :, :, 2 * D :], o_sem.at[k])
        for k, (refs, place) in enumerate(((grad_m, core), (grad_o, 1 - core)))
    ]

    @pl.when(j == 0)
    def _():
        for copy in out_in:
            copy.start()
        fetch(j, start)
        fill(g_low, gm_in[meta[1], 0], gg_in[...])
        acc[...] = jnp.zeros_like(acc)
        e2[...] = jnp.zeros_like(e2)
        for copy in out_in:
            copy.wait()
        for i in range(4):
            w_out[:, 192 * i : 192 * i + 192] = o_buf[i // 2, :, i % 2, :, :192].reshape(D, 192)

        def body(k):
            r = rows(k)
            branch = mm(att_a[r], w_out[: D // 2]) + mm(att_b[r], w_out[D // 2 :])
            m = x_ref[r].astype(F32) + (branch + vec_ref[4:5])
            mid[r] = m
            u, i = unit(m)
            inv[r] = jnp.broadcast_to(i, (FFC, 128))
            n2[r] = (u * vec_ref[5:6] + vec_ref[6:7]).astype(BF)

        each(ROWS // FFC, body)

    @pl.when(j < 4)
    def _():
        slot = j % 2
        fetch(j, wait)
        pl.when(j < 3)(lambda: fetch(j + 1, start))
        pl.when(j >= 2)(lambda: flush(j - 2, wait))
        dub_ref[j] = jnp.zeros((1, D), F32)

        def body(k):
            r = rows(k)
            for c in range(0, D, SUB):
                cols = slice(c, c + SUB)
                up = w_buf[slot, :, :, cols].reshape(D, SUB)
                down = w_buf[slot, c // 192 : (c + SUB) // 192, :, D:].reshape(SUB, D)
                h = mm(n2[r], up) + ub_ref[j, :, cols]
                t = mm_nt(g_low[r], down)
                phi = 0.5 + 0.5 * erf(h * math.sqrt(0.5))
                act[r, cols] = (h * phi).astype(BF)
                slope = phi + h * (jnp.exp(h * h * -0.5) * (1.0 / math.sqrt(2.0 * math.pi)))
                t = (t * slope).astype(BF)
                gh[r, cols] = t
                dub_ref[j, :, cols] += jnp.sum(t.astype(F32), axis=0, keepdims=True)
            acc[r] += mm(act[r], w_buf[slot, :, :, D:].reshape(D, D))
            e2[r] += mm_nt(gh[r], w_buf[slot, :, :, :D].reshape(D, D))

        each(ROWS // FFC, body)

        def grads(k):
            c = pl.multiple_of(k * SUB, SUB)
            t = mm_tn(act[:, pl.ds(c, SUB)], g_low[...]).astype(BF)
            g_buf[slot, pl.ds(k * (SUB // 192), SUB // 192), :, D:] = t.reshape(-1, 192, D)
            t = mm_tn(n2[...], gh[:, pl.ds(c, SUB)]).astype(BF)
            g_buf[slot, :, :, pl.ds(c, SUB)] = t.reshape(4, 192, SUB)

        each(D // SUB, grads)
        flush(j, start)

    @pl.when(j == 4)
    def _():
        flush(j - 2, wait)
        sums_ref[...] = jnp.zeros_like(sums_ref)

        def body(k):
            r = rows(k)
            m = mid[r]
            res = (m + (acc[r] + vec_ref[7:8])).astype(BF)
            keep_ref[...] = res[:TOK]
            send_ref[...] = res[HALF : HALF + TOK]
            g = g_low[r].astype(F32)
            e = e2[r]
            i = inv[r][:, 0:1]
            u = (m - jnp.mean(m, axis=-1, keepdims=True)) * i
            grad = g + norm_back(e, u, i, vec_ref[5:6])
            gm_ref[r] = grad
            low = grad.astype(BF)
            n2[r] = low
            ga_ref[r] = mm_nt(low, w_out[...]).astype(BF)
            for q, t in enumerate((low.astype(F32), e * u, e, g)):
                sums_ref[q : q + 1] += jnp.sum(t, axis=0, keepdims=True)

        each(ROWS // FFC, body)
        grad_out = jnp.concatenate([mm_tn(att[...], n2[...]) for att in (att_a, att_b)])
        grad_out = grad_out.astype(BF)
        for i in range(4):
            part = grad_out[:, 192 * i : 192 * i + 192].reshape(4, 192, 192)
            o_buf[i // 2, :, i % 2, :, :192] = part
            o_buf[i // 2, :, i % 2, :, 192:] = jnp.zeros((4, 192, 64), BF)
        for copy in out_back:
            copy.start()
        flush(j - 1, wait)
        for copy in out_back:
            copy.wait()


def ff(meta, x, att, cot, cot_got, mine, other, vec, up_bias):
    any_ref = pl.BlockSpec(memory_space=pl.ANY)
    wide = (any_ref, sds((4, 2, 192, 1792), BF))
    half = (whole((TOK, D)), sds((TOK, D), BF))
    ins = [(FULL, x)] + [(whole((ROWS, D // 2)), part) for part in att]
    ins += [(whole((2, 1, TOK, D)), cot), (whole((TOK, D)), cot_got)]
    ins += [(whole((16, D)), vec), (whole((4, 1, D)), up_bias)]
    ins += [(any_ref, piece) for piece in (*mine, *other)]
    outs = [half, half, (FULL, sds((ROWS, D), F32)), (FULL, sds((ROWS, D), BF)), wide, wide]
    outs += [(whole((8, D)), sds((8, D), F32)), (whole((4, 1, D)), sds((4, 1, D), F32))]
    return call(
        ff_kernel,
        meta,
        (5,),
        ins,
        outs,
        [pltpu.VMEM((ROWS, D), F32), pltpu.VMEM((ROWS, 128), F32), pltpu.VMEM((ROWS, D), BF)]
        + [pltpu.VMEM((ROWS, D), BF)] * 2
        + [pltpu.VMEM((ROWS, D), F32)] * 2
        + [pltpu.VMEM((ROWS, D), BF), pltpu.VMEM((D, D), BF)]
        + [pltpu.VMEM((2, 4, 192, 2 * D), BF)] * 2
        + [pltpu.VMEM((2, 4, 2, 192, 256), BF)]
        + [pltpu.SemaphoreType.DMA((2, 4)), pltpu.SemaphoreType.DMA((2,)), pltpu.SemaphoreType.DMA((10,))],
        us=36,
        vmem=VFF,
    )


def b1_kernel(
    meta, x_ref, n1_ref, gm_ref, qa_ref, ka_ref, va_ref, qb_ref, kb_ref, vb_ref, wm_ref, wo_ref, vec_ref, small_ref,
    keep_ref, send_ref, gwm_ref, gwo_ref, gj, e1,
):
    j = pl.program_id(0)
    core = meta[0]

    @pl.when(j == 0)
    def _():
        gj[0, :, 0:384] = qa_ref[...]
        gj[0, :, 384:640] = qb_ref[:, 0:256]
        gj[1, :, 0:128] = qb_ref[:, 256:384]
        gj[1, :, 128:512] = ka_ref[...]
        gj[1, :, 512:640] = kb_ref[:, 0:128]
        gj[2, :, 0:256] = kb_ref[:, 128:384]
        gj[2, :, 256:640] = va_ref[...]
        gj[3, :, 0:384] = vb_ref[...]
        gj[3, :, 384:640] = jnp.zeros((ROWS, 256), BF)
        e1[...] = jnp.zeros_like(e1)

    b = gj[j]

    def block(w_ref, grad_ref):
        e1[...] += mm_nt(b, rows_of(w_ref))
        grad_ref[:, 0] = mm_tn(n1_ref[...], b).astype(BF).reshape(4, 192, 640)

    own = (j // 2) == core
    pl.when(own)(lambda: block(wm_ref, gwm_ref))
    pl.when(jnp.logical_not(own))(lambda: block(wo_ref, gwo_ref))

    @pl.when(j == 3)
    def _():
        tot = [None] * 4
        for c in range(2):
            r = slice(c * HALF, (c + 1) * HALF)
            u, i = unit(x_ref[r].astype(F32))
            e = e1[r]
            grad = gm_ref[r] + norm_back(e, u, i, vec_ref[0:1])
            if c == 0:
                keep_ref[...] = grad[:TOK]
            else:
                send_ref[...] = grad[:TOK].astype(BF)
            sides = [
                jnp.concatenate([left[r], right[r]], axis=1).astype(F32)
                for left, right in ((qa_ref, qb_ref), (va_ref, vb_ref))
            ]
            for k, t in enumerate((e * u, e, *sides)):
                t = jnp.sum(t, axis=0, keepdims=True)
                tot[k] = t if c == 0 else tot[k] + t
        rows = jnp.concatenate(tot + [small_ref[4:16], jnp.zeros((112, D), F32)], axis=0)
        cols = rows.T.astype(BF)

        def put(ref):
            ref[:, 0, :, 384:512] = cols.reshape(4, 192, 128)

        pl.when(core == 1)(lambda: put(gwm_ref))
        pl.when(core == 0)(lambda: put(gwo_ref))


def b1(meta, x, n1, gm, low, high, mine, other, vec, small):
    pair = [(spec(640), sds((4, 2, 192, 640), BF)) for spec in (mine_spec, other_spec)]
    return call(
        b1_kernel,
        meta,
        (4,),
        [(FULL, x), (FULL, n1), (FULL, gm)]
        + [(whole((ROWS, D // 2)), part) for part in (*low, *high)]
        + [(mine_spec(640), mine), (other_spec(640), other), (whole((16, D)), vec), (whole((16, D)), small)],
        [(whole((TOK, D)), sds((TOK, D), F32)), (whole((TOK, D)), sds((TOK, D), BF))] + pair,
        [pltpu.VMEM((4, ROWS, 640), BF), pltpu.VMEM((ROWS, D), F32)],
        us=12,
    )


def ring_groups(axis_zero, axis_one):
    groups = []
    for core, axis in ((0, axis_zero), (1, axis_one)):
        others = [name for name in "zxy" if name != axis]
        for i in range(4):
            for j in range(4):
                at = {others[0]: i, others[1]: j}
                line = []
                for k in range(4):
                    at[axis] = k
                    z, x, y = at["z"], at["x"], at["y"]
                    line.append((((z * 2 + x // 2) * 4 + y) * 2 + core) * 2 + x % 2)
                groups.append(line)
    return groups


ZY = ring_groups("z", "y")
YZ = ring_groups("y", "z")


def swap(value, axis):
    return lax.ppermute(value, axis, [(0, 1), (1, 0)])


def tie(*values):
    return lax.optimization_barrier(values)


CROSS = [(4 * i + k, 4 * k + i) for i in range(4) for k in range(4)]


def cross(value):
    return lax.ppermute(value, ("z", "y"), CROSS)


def along(value, groups):
    return lax.all_to_all(value, AXES, 0, 0, tiled=True, axis_index_groups=groups)


def copies(value, groups):
    return along(jnp.broadcast_to(value[None], (4, *value.shape)), groups)


def step_along(value, groups, step):
    pairs = [(line[i], line[(i + step) % 4]) for line in groups for i in range(4)]
    return lax.ppermute(value, AXES, pairs)


def among(value):
    return lax.all_to_all(value, ("core", "xh", "xl"), 0, 0, tiled=True)


def per_device(
    inputs,
    cotangent,
    lengths,
    w_qkv,
    w_out,
    w_up,
    w_down,
    ln1_gain,
    ln1_shift,
    q_bias,
    v_bias,
    out_bias,
    ln2_gain,
    ln2_shift,
    up_bias,
    down_bias,
):
    side = lax.axis_index("xl")
    core = lax.axis_index("core")

    def theirs(block):
        return swap(lax.dynamic_index_in_dim(block, 1 - side, 0, keepdims=False)[0], "xl")

    def give_back(kept, got):
        got = got.astype(kept.dtype)
        first = side == 0
        return jnp.stack([jnp.where(first, kept, got), jnp.where(first, got, kept)])[:, None]

    got_image = theirs(inputs)

    row = lax.broadcasted_iota(jnp.int32, (12, 6), 0)
    smalls = jnp.pad(up_bias.reshape(4, 6), ((8, 0), (0, 0)))
    for i, part in enumerate(
        (ln1_gain, ln1_shift, q_bias, v_bias, out_bias, ln2_gain, ln2_shift, down_bias)
    ):
        smalls = jnp.where(row == i, part[None], smalls)
    wide_one = jnp.concatenate([w_qkv, smalls.T, jnp.zeros((6, 244), BF)], axis=1)
    cut_out = jnp.pad(w_out.reshape(6, 4, 192), ((0, 0), (0, 0), (0, 64)))
    cut_up = w_up.reshape(6, 32, 4, 24).transpose(0, 2, 1, 3).reshape(6, 4, D)
    cut = jnp.concatenate([wide_one.reshape(6, 4, 640), cut_up, cut_out], axis=2)
    cut = jnp.moveaxis(cut, 1, 0).reshape(2, 12, 1664)
    cut = jnp.concatenate([cut, jnp.stack([w_down.reshape(12, 2 * D)] * 2)], axis=2)
    sent = jnp.stack([cut[0]] * 4 + [cross(cut[1])] * 4)
    line = among(sent)
    blocks = line[..., :1664].reshape(2, 2, 2, 2, 6, 1664).transpose(3, 1, 0, 2, 4, 5)
    downs = lax.dynamic_index_in_dim(line.reshape(2, 2, 2, 12, 3200), core, 0, keepdims=False)
    downs = downs[..., 1664:].reshape(2, 2, 24, D).transpose(1, 0, 2, 3)
    blocks = blocks.reshape(2, 2, 24, 1664)
    line = jnp.concatenate([blocks[..., :1408], downs, blocks[..., 1408:]], axis=3)
    plane = copies(line, YZ).transpose(1, 2, 0, 3, 4).reshape(384, 2432)
    plane, got_image = tie(plane, got_image)
    one_mine = copies(plane[:, :640], ZY).reshape(4, 2, 192, 640)
    own = plane[:, 640:].reshape(2, 192, 1792)
    got_cotangent = theirs(cotangent)
    length = lax.dynamic_index_in_dim(lengths, side, 0, keepdims=False)[0]
    z, y = lax.axis_index("z"), lax.axis_index("y")
    at_mine, at_other = jnp.where(core == 0, z, y), jnp.where(core == 0, y, z)
    meta = jnp.stack([core, side, length, at_mine, at_other]).astype(jnp.int32)
    own, one_mine, got_cotangent, meta = tie(own, one_mine, got_cotangent, meta)
    one_other = swap(one_mine, "core")
    before, after = step_along(own, ZY, 1), step_along(own, ZY, 3)

    qkv, normed, vecs, image = f1(meta, inputs, got_image, one_mine, one_other)
    att_low, total_low = f2(meta, qkv, 0)
    before, after, qkv, att_low = tie(before, after, qkv, att_low)
    far_low, far_high = step_along(before[0], ZY, 1), step_along(after[1], ZY, 3)
    near = [swap(part, "core") for part in (own, after, before)]
    att_high, total_high = f2(meta, qkv, 3)
    far_low, far_high, att_high, *near = tie(far_low, far_high, att_high, *near)
    mine = (own, after, far_low, far_high, before)
    other = (near[0], near[1], swap(far_low, "core"), swap(far_high, "core"), near[2])
    up_order = vecs[8:12].reshape(4, 32, 4, 6).transpose(2, 1, 0, 3).reshape(4, 1, D)

    att_high, up_order = tie(att_high, up_order)
    (
        kept_result,
        sent_result,
        grad_middle,
        grad_attended,
        wide_kept,
        wide_away,
        sums,
        up_sums,
    ) = ff(
        meta,
        image,
        (att_low, att_high),
        cotangent,
        got_cotangent,
        mine,
        other,
        vecs,
        up_order,
    )

    got_wide = swap(wide_away, "core")
    low = b2(meta, qkv, grad_attended, att_low, total_low, 0)
    got_wide, *low = tie(got_wide, *low)
    two = (wide_kept.astype(F32) + got_wide.astype(F32)).astype(BF)
    two, grad_attended = tie(two, grad_attended)
    two = along(two, ZY)

    high = b2(meta, qkv, grad_attended, att_high, total_high, 3)
    sent_result, up_sums, sums, *high = tie(sent_result, up_sums, sums, *high)
    got_result = swap(sent_result, "xl")
    up_sums = up_sums.reshape(4, 32, 4, 6).transpose(2, 1, 0, 3).reshape(4, D)
    small_sums = jnp.concatenate(
        [jnp.zeros((4, D), F32), sums[:4], up_sums, jnp.zeros((4, D), F32)]
    )
    kept_grad, sent_grad, one_kept, one_away = b1(
        meta, image, normed, grad_middle, low, high, one_mine, one_other, vecs, small_sums
    )
    one_kept, one_away, got_result = tie(one_kept, one_away, got_result)
    one = (one_kept.astype(F32) + swap(one_away, "core").astype(F32)).astype(BF)
    one, two = tie(one, two)
    one = along(one, ZY)

    def shrink(parts):
        return jnp.sum(parts.astype(F32), axis=0).astype(BF)

    def plane_of(parts):
        return shrink(parts).reshape(2, 2, 4, 24, parts.shape[-1]).transpose(2, 0, 1, 3, 4)

    two = plane_of(two)
    place = at_other

    def piece(step):
        part = lax.dynamic_index_in_dim(two, (place + step) % 4, 0, keepdims=False)
        if step:
            part = step_along(part, YZ, step)
        return part

    parts = [piece(step) for step in range(4)]
    one = along(plane_of(one), YZ)
    one, *parts = tie(one, *parts)
    one = shrink(one)
    two = sum(part.astype(F32) for part in parts).astype(BF)
    line = jnp.concatenate([one, two], axis=3)
    blocks = jnp.concatenate([line[..., :1408], line[..., 2176:]], axis=3)
    blocks = blocks.reshape(2, 2, 2, 2, 6, 1664).transpose(2, 1, 3, 0, 4, 5).reshape(8, 12, 1664)
    downs = line[..., 1408:2176].transpose(1, 0, 2, 3).reshape(1, 4, 12, 2 * D)
    downs = jnp.concatenate([downs, downs]).reshape(8, 12, 2 * D)
    got = among(jnp.concatenate([blocks, downs], axis=2)).reshape(2, 4, 12, 3200)
    got = jnp.sum(got.astype(F32), axis=1)
    high = cross(got[1].astype(BF)).astype(F32)
    own_down = jnp.where(core == 0, got[0, :, 1664:], high[:, 1664:]).reshape(24, D)
    back = jnp.stack([got[0, :, :1664], high[:, :1664]]).reshape(4, 6, 1664)
    own_one = jnp.moveaxis(back[..., :640], 0, 1).reshape(6, 2560)
    own_up = back[..., 640:1408].reshape(4, 6, 32, 24).transpose(1, 2, 0, 3).reshape(6, FF)
    own_out = jnp.moveaxis(back[..., 1408:1600], 0, 1).reshape(6, D)
    small = own_one[:, 3 * D : 3 * D + 12].T
    return (
        give_back(kept_result, got_result),
        give_back(kept_grad, swap(sent_grad, "xl")),
        own_one[:, : 3 * D],
        own_out,
        own_up,
        own_down,
        small[0],
        small[1],
        small[2],
        small[3],
        small[4],
        small[5],
        small[6],
        small[8:].reshape(24),
        small[7],
    )


def solution(mesh):
    fine = Mesh(mesh.devices.reshape(4, 2, 4, 2, 2), AXES)
    images = ("z", "xh", "y", "core")
    rows, vec = P(AXES, None), P(AXES)
    tokens = P(None, images, "xl", None)
    return jax.shard_map(
        per_device,
        mesh=fine,
        in_specs=(tokens, tokens, P(None, images)) + (rows,) * 4 + (vec,) * 9,
        out_specs=(tokens, tokens) + (rows,) * 4 + (vec,) * 9,
        check_vma=False,
    )
```
